256 devices in a mesh: bond: 32 (over z, y), mpo: 8 (over x, core).
Axes of the slice: x: 4, y: 4, z: 8, core: 2. Of those that a mesh axis runs over, the one named last changes fastest.
Arguments:
- wavefunction: bfloat16 [2048, 128, 128], P('bond'), may hold values from -6 to 6
- left_environment: bfloat16 [40, 512, 128, 128], P('mpo', 'bond'), may hold values from -0.5 to 0.5
- right_environment: bfloat16 [40, 512, 128, 128], P('mpo', 'bond'), may hold values from -0.078125 to 0.078125
- right_sector: int32 [2048], P('bond'), may hold values from 0 to 511, as said below
Outputs:
- product: bfloat16 [2048, 128, 128], P('bond', 'mpo')
The draws below stay inside these ranges and needn't reach their ends.
Inputs may be any that keep to these rules, and one draw needn't show every extreme that they name: `right_sector`: sector s is owned by index s // 16 of bond. Among the blocks of one device (aligned runs of 64 blocks), at most 3 name right sectors of one owner; in every draw one owner receives exactly 3 from every run.
All inputs are finite; a program needn't handle non-finite values.
Results may differ from the reference program's by a relative error of at most 0.005.
Values may be sent and summed in bfloat16 or wider, within the bound.
No kernel may reach another device: no remote copies, remote signals or barrier semaphores. Data moves between devices by JAX's collectives and lax.ppermute only.
A program may use at most 128 MiB of HBM per device.

```python
import jax
import jax.numpy as jnp
from jax import lax

BLOCK = 128
MPO = 40
SEC_DEV = 16
GROUP = 4
SECTORS = 512
BLK_DEV = 64
BLOCKS = 2048
CAP = 3
N_BOND = 32


def draw_right_sector(key, part):
    key = jax.random.fold_in(key, 11)
    first = jax.random.fold_in(key, 0)
    third = jax.random.fold_in(key, 2)
    busiest = jax.random.randint(first, (), 0, N_BOND)

    def one_device(device_key):
        key_order, key_shuffle, key_local = jax.random.split(device_key, 3)
        order = jax.random.permutation(key_order, N_BOND * CAP)
        priority = jnp.where(order // CAP == busiest, 0, 1)
        ranked = order[jnp.argsort(priority, stable=True)]
        owners = ranked[:BLK_DEV] // CAP
        owners = jax.random.permutation(key_shuffle, owners)
        local = jax.random.randint(key_local, (BLK_DEV,), 0, SEC_DEV)
        return owners * SEC_DEV + local
    device_keys = jax.random.split(third, N_BOND)
    return jax.vmap(one_device)(device_keys).reshape(-1).astype(jnp.int32)


def shard_levels(stream_key, extent, cuts, least, high):
    loudness, own = 1.0, jax.random.fold_in(stream_key, 6)
    for dim, parts in cuts:
        draws = jnp.exp(jax.random.uniform(jax.random.fold_in(own, dim), (parts,), jnp.float32, least / len(cuts), high / len(cuts)))
        loudness = loudness * jnp.repeat(draws, extent[dim] // parts).reshape([-1 if axis == dim else 1 for axis in range(len(extent))])
    return loudness


def bell_draw(rng, dims, scale, bound, cuts=(), kind=jnp.bfloat16):
    array = scale * jax.random.normal(rng, dims, jnp.float32)
    if cuts:
        array = array * shard_levels(rng, dims, cuts, -0.22, 0.18)
    return jnp.clip(array, -bound, bound).astype(kind)


def setup_inputs(seed: int = 0) -> dict:
    key_of = jax.random.split(jax.random.key(seed), 5)
    wavefunction = bell_draw(key_of[0], (BLOCKS, BLOCK, BLOCK), 1.0, 6.0, ((0, 32),))
    left_environment = bell_draw(key_of[1], (MPO, SECTORS, BLOCK, BLOCK), BLOCK ** -0.5, 0.5, ((0, 8), (1, 32)))
    right_environment = bell_draw(key_of[2], (MPO, SECTORS, BLOCK, BLOCK), (BLOCK * MPO) ** -0.5, 0.078125, ((0, 8), (1, 32)))
    right_sector = draw_right_sector(jax.random.fold_in(key_of[4], 71), 0)
    return dict(wavefunction=wavefunction, left_environment=left_environment, right_environment=right_environment, right_sector=right_sector)


def reference(wavefunction, left_environment, right_environment, right_sector):
    grouped = wavefunction.astype(jnp.float32).reshape(SECTORS, GROUP, BLOCK, BLOCK)

    def one_term(total, environments):
        left_block, right_block = environments
        mixed = jnp.einsum("sij,sgjl->sgil", left_block.astype(jnp.float32), grouped)
        mixed = mixed.astype(jnp.bfloat16).reshape(BLOCKS, BLOCK, BLOCK)
        chosen = jnp.take(right_block.astype(jnp.float32), right_sector, axis=0)
        total = total + jnp.einsum("kil,kml->kim", mixed.astype(jnp.float32), chosen)
        return total, None

    start = jnp.zeros((BLOCKS, BLOCK, BLOCK), jnp.float32)
    total, unused = lax.scan(one_term, start, (left_environment, right_environment))
    return total.astype(jnp.bfloat16)
```

```python
import functools

import jax
import jax.numpy as jnp
from jax import lax
from jax.experimental import pallas as pl
from jax.experimental.pallas import tpu as pltpu
from jax.sharding import Mesh, PartitionSpec as P

Z, Y, M = 8, 4, 8
CAP = 3
SLOTS = Z * CAP
OFFSETS = (0, -1, 1, -2, 2, -3, 3, 4)
RANK = tuple(OFFSETS.index(((d + 3) % Z) - 3) for d in range(Z))
RIGHT = [(i, (i + 1) % Z) for i in range(Z)]
LEFT = [(i, (i - 1) % Z) for i in range(Z)]


def multiply_kernel(places, per_place, info_ref, *refs):
    count = len(places)
    slots = count * CAP
    psi = refs[:count]
    left = refs[count : count + slots]
    right = refs[count + slots : count + slots + slots * per_place]
    out_ref = refs[-1]
    home = pl.program_id(0)
    terms = left[0].shape[1]
    width = left[0].shape[-1]
    for p in range(count):
        for c in range(CAP):
            s = p * CAP + c
            blocks = left[s][0, :, 0].reshape(terms * width, width)
            mixed = jnp.dot(blocks, psi[p][0, c], preferred_element_type=jnp.float32)
            mixed = mixed.astype(jnp.bfloat16)
            mixed = jnp.concatenate(
                [mixed[w * width : (w + 1) * width] for w in range(terms)], axis=1
            )
            if per_place == 1:
                chosen = right[s][:, 0]
            else:
                half = right[2 * s].shape[1]
                sector = info_ref[home * SLOTS + places[p] * CAP + c] % 16
                chosen = jnp.where(sector < 8, right[2 * s][:, 0], right[2 * s + 1][:, 0])
            chosen = jnp.concatenate([chosen[w] for w in range(terms)], axis=1)
            total = lax.dot_general(
                mixed, chosen, (((1,), (1,)), ((), ())), preferred_element_type=jnp.float32
            )
            out_ref[0, :, s] = total.astype(jnp.bfloat16).reshape(M, width // M, width)


def multiply(places, info, psi, left, rights):
    terms, width = left.shape[1], left.shape[-1]
    slots = len(places) * CAP
    per_place = 2 if isinstance(rights[0], tuple) else 1
    in_specs, operands = [], []
    for p in places:
        in_specs.append(pl.BlockSpec((1, CAP, width, width), lambda h, info, p=p: (h, p, 0, 0)))
        operands.append(psi)
    for p in places:
        for c in range(CAP):
            q = p * CAP + c
            in_specs.append(
                pl.BlockSpec(
                    (1, terms, 1, width, width),
                    lambda h, info, q=q: (h, 0, info[h * SLOTS + q] // 16, 0, 0),
                )
            )
            operands.append(left)
    for i, p in enumerate(places):
        for c in range(CAP):
            q = p * CAP + c
            if per_place == 1:
                in_specs.append(
                    pl.BlockSpec(
                        (terms, 1, width, width),
                        lambda h, info, q=q: (0, info[h * SLOTS + q] % 16, 0, 0),
                    )
                )
                operands.append(rights[i])
            else:
                low, high = rights[i]
                in_specs.append(
                    pl.BlockSpec(
                        (terms, 1, width, width),
                        lambda h, info, q=q: (0, jnp.minimum(info[h * SLOTS + q] % 16, 7), 0, 0),
                    )
                )
                in_specs.append(
                    pl.BlockSpec(
                        (terms, 1, width, width),
                        lambda h, info, q=q: (0, jnp.maximum(info[h * SLOTS + q] % 16, 8) - 8, 0, 0),
                    )
                )
                operands += [low, high]
    flops = 2 * 2 * Y * slots * terms * width**3
    moved = Y * slots * (2 * terms + 2) * width * width * 2
    return pl.pallas_call(
        functools.partial(multiply_kernel, tuple(places), per_place),
        out_shape=jax.ShapeDtypeStruct((Y, M, slots, width // M, width), jnp.bfloat16),
        grid_spec=pltpu.PrefetchScalarGridSpec(
            num_scalar_prefetch=1,
            grid=(Y,),
            in_specs=in_specs,
            out_specs=pl.BlockSpec(
                (1, M, slots, width // M, width), lambda h, info: (h, 0, 0, 0, 0)
            ),
        ),
        compiler_params=pltpu.CompilerParams(vmem_limit_bytes=40 * 1024 * 1024),
        cost_estimate=pl.CostEstimate(flops=flops, bytes_accessed=moved, transcendentals=0),
    )(info, *operands)


def on_device(wavefunction, left_environment, right_environment, right_sector):
    here = lax.axis_index("z")
    blocks = wavefunction.shape[0]
    owned = left_environment.shape[1]
    members = blocks // owned

    from_left, from_right = right_environment, right_environment
    arrived = [right_environment]
    for _ in range(3):
        from_left = lax.ppermute(from_left, "z", RIGHT)
        from_right = lax.ppermute(from_right, "z", LEFT)
        arrived += [from_left, from_right]
    half = owned // 2
    low = lax.ppermute(from_left[:, :half], "z", RIGHT)
    high = lax.ppermute(from_right[:, half:], "z", LEFT)
    arrived.append((low, high))

    lefts = lax.all_gather(left_environment, "y", axis=0, tiled=False)

    owner = right_sector // owned
    same = owner[:, None] == owner[None, :]
    index = jnp.arange(blocks, dtype=jnp.int32)
    place = jnp.sum((same & (index[None, :] < index[:, None])).astype(jnp.int32), axis=1)
    offset = (owner // Y - here) % Z
    rank = jnp.sum(
        jnp.where(offset[:, None] == jnp.arange(Z)[None, :], jnp.array(RANK, jnp.int32)[None, :], 0),
        axis=1,
    )
    slot = (owner % Y) * SLOTS + rank * CAP + place
    filled = slot[None, :] == jnp.arange(Y * SLOTS, dtype=jnp.int32)[:, None]
    source = jnp.sum(jnp.where(filled, index[None, :], 0), axis=1)
    detail = (index // members) * 16 + right_sector % owned
    detail = jnp.sum(jnp.where(filled, detail[None, :], 0), axis=1)
    outgoing = wavefunction.at[source].get(mode="promise_in_bounds").reshape((Y, SLOTS) + wavefunction.shape[1:])
    psi = lax.all_to_all(outgoing, "y", split_axis=0, concat_axis=0, tiled=True)
    info = lax.all_to_all(detail.reshape(Y, SLOTS), "y", split_axis=0, concat_axis=0, tiled=True)
    info = info.reshape(-1)

    picks = filled.T.astype(jnp.bfloat16).reshape(blocks, Y, SLOTS)
    total = jnp.zeros((), jnp.float32)
    for places in ((0, 1, 2, 3, 4), (5, 6), (7,)):
        part = multiply(places, info, psi, lefts, [arrived[p] for p in places])
        part = part.reshape((Y * M,) + part.shape[2:])
        part = lax.all_to_all(part, ("y", "mpo"), split_axis=0, concat_axis=0, tiled=True)
        part = part.reshape((Y, M) + part.shape[1:]).astype(jnp.float32).sum(axis=1)
        part = part.astype(jnp.bfloat16)
        pick = picks[:, :, places[0] * CAP : (places[-1] + 1) * CAP]
        total = total + jnp.einsum("kys,ysil->kil", pick, part, preferred_element_type=jnp.float32)
    return total.astype(jnp.bfloat16)


def solution(mesh):
    fine = Mesh(mesh.devices.reshape(Z, Y, M), ("z", "y", "mpo"))
    bond = ("z", "y")
    placed = (
        P(bond, None, None),
        P("mpo", bond, None, None),
        P("mpo", bond, None, None),
        P(bond),
    )
    return jax.shard_map(
        on_device, mesh=fine, in_specs=placed, out_specs=P(bond, "mpo", None), check_vma=False
    )
```

```python
import functools

import jax
import jax.numpy as jnp
from jax import lax
from jax.experimental import pallas as pl
from jax.experimental.pallas import tpu as pltpu
from jax.sharding import Mesh, PartitionSpec as P

Z, Y, X, C = 8, 4, 4, 2
M = X * C
CAP = 3
SLOTS = Z * CAP
OFFSETS = (0, -1, 1, -2, 2, -3, 3, 4)
RANK = tuple(OFFSETS.index(((d + 3) % Z) - 3) for d in range(Z))
RIGHT = [(i, (i + 1) % Z) for i in range(Z)]
LEFT = [(i, (i - 1) % Z) for i in range(Z)]


def left_products(blocks, psi):
    terms, width = blocks.shape[0], blocks.shape[-1]
    mixed = jnp.dot(
        blocks.reshape(terms * width, width), psi, preferred_element_type=jnp.float32
    ).astype(jnp.bfloat16)
    return jnp.concatenate([mixed[w * width : (w + 1) * width] for w in range(terms)], axis=1)


def times_right(mixed, chosen):
    total = lax.dot_general(
        mixed,
        jnp.concatenate([chosen[w, 0] for w in range(chosen.shape[0])], axis=1),
        (((1,), (1,)), ((), ())),
        preferred_element_type=jnp.float32,
    )
    width = total.shape[0]
    return total.astype(jnp.bfloat16).reshape(M, width // M, width)


def near_kernel(count, info_ref, *refs):
    slots = count * CAP
    psi = refs[:count]
    left = refs[count : count + slots]
    right = refs[count + slots : -1]
    out_ref = refs[-1]
    for s in range(slots):
        mixed = left_products(left[s][0, :, 0], psi[s // CAP][0, s % CAP])
        out_ref[0, :, s] = times_right(mixed, right[s])


def prepare_kernel(counts, info_ref, *refs):
    count = sum(counts)
    psi = refs[:count]
    left = refs[count : count + count * CAP]
    outs = refs[count + count * CAP :]
    s = 0
    for out_ref, n in zip(outs, counts):
        for i in range(n * CAP):
            out_ref[0, i] = left_products(left[s][0, :, 0], psi[s // CAP][0, s % CAP])
            s += 1


def far_kernel(info_ref, mixed_ref, *refs):
    for s in range(mixed_ref.shape[1]):
        refs[-1][0, :, s] = times_right(mixed_ref[0, s], refs[s])


def end_kernel(low_mixed, high_mixed, low, high, out_ref):
    for s in range(CAP):
        out_ref[0, 0, :, s] = times_right(low_mixed[0, s], low[:, s : s + 1])
        out_ref[1, 0, :, s] = times_right(high_mixed[0, s], high[:, s : s + 1])


def fetch_kernel(low_index, high_index, low_ref, high_ref, low_out, high_out):
    low_out[...] = low_ref[...]
    high_out[...] = high_ref[...]


PARAMS = pltpu.CompilerParams(vmem_limit_bytes=60 * 1024 * 1024)


def cost(slots, matmuls, terms, width):
    return pl.CostEstimate(
        flops=2 * slots * matmuls * terms * width**3,
        bytes_accessed=slots * (matmuls * terms + 2) * width * width * 2,
        transcendentals=0,
    )


def psi_and_left(places, psi, left):
    terms, width = left.shape[1], left.shape[-1]
    specs, operands = [], []
    for p in places:
        side, at = divmod(p, Z // C)
        specs.append(pl.BlockSpec((1, CAP, width, width), lambda h, info, at=at: (h, at, 0, 0)))
        operands.append(psi[side])
    for p in places:
        for q in range(p * CAP, (p + 1) * CAP):
            specs.append(
                pl.BlockSpec(
                    (1, terms, 1, width, width),
                    lambda h, info, q=q: (h, 0, info[h * SLOTS + q] // 16, 0, 0),
                )
            )
            operands.append(left)
    return specs, operands


def rights(places, arrived):
    specs, operands = [], []
    for p in places:
        for q in range(p * CAP, (p + 1) * CAP):
            terms, _, rows, width = arrived[p].shape
            specs.append(
                pl.BlockSpec(
                    (terms, 1, rows, width),
                    lambda h, info, q=q: (0, info[h * SLOTS + q] % 16, 0, 0),
                )
            )
            operands.append(arrived[p])
    return specs, operands


def product_shape(slots, width):
    out = jax.ShapeDtypeStruct((Y, M, slots, width // M, width), jnp.bfloat16)
    spec = pl.BlockSpec((1, M, slots, width // M, width), lambda h, info: (h, 0, 0, 0, 0))
    return out, spec


def near_products(places, info, psi, left, arrived):
    terms, width = left.shape[1], left.shape[-1]
    slots = len(places) * CAP
    specs, operands = psi_and_left(places, psi, left)
    more_specs, more = rights(places, arrived)
    out, out_spec = product_shape(slots, width)
    return pl.pallas_call(
        functools.partial(near_kernel, len(places)),
        out_shape=out,
        grid_spec=pltpu.PrefetchScalarGridSpec(
            num_scalar_prefetch=1, grid=(Y,), in_specs=specs + more_specs, out_specs=out_spec
        ),
        compiler_params=PARAMS,
        cost_estimate=cost(Y * slots, 2, terms, width),
    )(info, *operands, *more)


def prepare(groups, info, psi, left):
    terms, width = left.shape[1], left.shape[-1]
    specs, operands = psi_and_left(sum(groups, ()), psi, left)
    counts = tuple(len(g) for g in groups)
    return pl.pallas_call(
        functools.partial(prepare_kernel, counts),
        out_shape=[
            jax.ShapeDtypeStruct((Y, n * CAP, width, terms * width), jnp.bfloat16) for n in counts
        ],
        grid_spec=pltpu.PrefetchScalarGridSpec(
            num_scalar_prefetch=1,
            grid=(Y,),
            in_specs=specs,
            out_specs=[
                pl.BlockSpec((1, n * CAP, width, terms * width), lambda h, info: (h, 0, 0, 0))
                for n in counts
            ],
        ),
        compiler_params=PARAMS,
        cost_estimate=cost(Y * sum(counts) * CAP, 1, terms, width),
    )(info, *operands)


def far_products(places, info, mixed, arrived):
    slots, width = mixed.shape[1:3]
    terms = mixed.shape[3] // width
    specs, operands = rights(places, arrived)
    out, out_spec = product_shape(slots, width)
    mixed_spec = pl.BlockSpec((1,) + mixed.shape[1:], lambda h, info: (h, 0, 0, 0))
    return pl.pallas_call(
        far_kernel,
        out_shape=out,
        grid_spec=pltpu.PrefetchScalarGridSpec(
            num_scalar_prefetch=1, grid=(Y,), in_specs=[mixed_spec] + specs, out_specs=out_spec
        ),
        compiler_params=PARAMS,
        cost_estimate=cost(Y * slots, 2, terms, width),
    )(info, mixed, *operands)


def end_products(mixed, sent):
    side = Y // 2
    slots, width = mixed.shape[1:3]
    low, high = sent
    terms = low.shape[0]
    part = pl.BlockSpec((terms, CAP) + low.shape[2:], lambda g: (0, g, 0, 0))
    out = pl.pallas_call(
        end_kernel,
        out_shape=jax.ShapeDtypeStruct((2, side, M, slots, width // M, width), jnp.bfloat16),
        grid=(side,),
        in_specs=[
            pl.BlockSpec((1,) + mixed.shape[1:], lambda g: (g, 0, 0, 0)),
            pl.BlockSpec((1,) + mixed.shape[1:], lambda g: (g + side, 0, 0, 0)),
            part,
            part,
        ],
        out_specs=pl.BlockSpec(
            (2, 1, M, slots, width // M, width), lambda g: (0, g, 0, 0, 0, 0)
        ),
        compiler_params=PARAMS,
        cost_estimate=cost(Y * slots, 2, terms, width),
    )(mixed, mixed, low, high)
    return out.reshape((Y,) + out.shape[2:])


def fetch(low, high, low_index, high_index):
    terms, _, rows, width = low.shape
    count = low_index.shape[0]
    block = (terms, 1, rows, width)
    out = jax.ShapeDtypeStruct((terms, count, rows, width), low.dtype)
    out_spec = pl.BlockSpec(block, lambda i, low_index, high_index: (0, i, 0, 0))
    return pl.pallas_call(
        fetch_kernel,
        out_shape=[out, out],
        grid_spec=pltpu.PrefetchScalarGridSpec(
            num_scalar_prefetch=2,
            grid=(count,),
            in_specs=[
                pl.BlockSpec(block, lambda i, low_index, high_index: (0, low_index[i], 0, 0)),
                pl.BlockSpec(block, lambda i, low_index, high_index: (0, high_index[i], 0, 0)),
            ],
            out_specs=[out_spec, out_spec],
        ),
        compiler_params=PARAMS,
        cost_estimate=pl.CostEstimate(
            flops=0, bytes_accessed=4 * terms * count * rows * width * 2, transcendentals=0
        ),
    )(low_index, high_index, low, high)


def exchange(part):
    part = part.reshape((Y * M,) + part.shape[2:])
    part = lax.all_to_all(part, ("y", "x", "c"), split_axis=0, concat_axis=0, tiled=True)
    return part.reshape((Y, M) + part.shape[1:])


def on_device(wavefunction, left_environment, right_environment, right_sector):
    z, y, core = (lax.axis_index(name) for name in ("z", "y", "c"))
    blocks, width = wavefunction.shape[:2]
    owned = left_environment.shape[1]
    members = blocks // owned
    tie = lax.optimization_barrier

    lefts = lax.all_gather(left_environment, "y", axis=0, tiled=False)
    beyond = lax.ppermute(right_sector, "z", LEFT)
    before = lax.ppermute(right_sector, "z", RIGHT)
    start, beyond, before = tie((right_environment, beyond, before))

    index = jnp.arange(blocks, dtype=jnp.int32)
    earlier = index[None, :] < index[:, None]

    def slots_of(sectors, plane):
        owner = sectors // owned
        same = owner[:, :, None] == owner[:, None, :]
        place = jnp.sum((same & earlier).astype(jnp.int32), axis=2)
        offset = (owner // Y - plane) % Z
        rank = sum(jnp.where(offset == d, RANK[d], 0) for d in range(Z))
        return owner % Y, rank * CAP + place

    def into(slots, values, count, start=0):
        hit = slots[:, None, :] == jnp.arange(start, start + count, dtype=jnp.int32)[None, :, None]
        return jnp.sum(jnp.where(hit, values[:, None, :], 0), axis=2)

    column, slot = slots_of(right_sector[None], z)
    slot = column * SLOTS + slot
    split = SLOTS // C
    mine = (slot // SLOTS) * split + jnp.where((slot % SLOTS) // split == core, slot % split, -Y * SLOTS)
    source = into(mine, index[None], Y * split)[0]
    outgoing = wavefunction.at[source].get(mode="promise_in_bounds")
    outgoing = outgoing.reshape((Y, split) + wavefunction.shape[1:])

    planes = jnp.broadcast_to(jnp.stack([right_sector, beyond, before]), (Y, 3, blocks))
    planes = lax.all_to_all(planes, "y", split_axis=0, concat_axis=0, tiled=True)

    def for_this_column(sectors, plane):
        column, slots = slots_of(sectors, plane)
        return jnp.where(column == y, slots, -1)

    info = into(
        for_this_column(planes[:, 0], z), (index // members) * 16 + planes[:, 0] % owned, SLOTS
    ).reshape(-1)
    low, high = planes[: Y // 2, 1], planes[Y // 2 :, 2]
    wanted = [
        into(for_this_column(low, z + 1), low % owned, CAP, SLOTS - CAP).reshape(-1),
        into(for_this_column(high, z - 1), high % owned, CAP, SLOTS - CAP).reshape(-1),
    ]

    def step(moving):
        return [lax.ppermute(moving[0], "z", RIGHT), lax.ppermute(moving[1], "z", LEFT)]

    first = step([start, start])
    psi = lax.all_to_all(outgoing, "y", split_axis=0, concat_axis=0, tiled=True)
    first, psi, info, wanted = tie((first, psi, info, wanted))
    second = step(first)
    other = lax.ppermute(psi, "c", [(0, 1), (1, 0)])
    psi = (jnp.where(core == 0, psi, other), jnp.where(core == 0, other, psi))
    second, psi = tie((second, psi))
    third = step(second)
    arrived = [start] + first + second + third
    near = near_products((0, 1, 2, 3, 4), info, psi, lefts, arrived)
    far_mixed, end_mixed = prepare(((5, 6), (7,)), info, psi, lefts)
    wanted, near, far_mixed, end_mixed = tie((wanted, near, far_mixed, end_mixed))
    fourth = step(fetch(*third, *wanted))
    near = exchange(near)
    far = far_products((5, 6), info, far_mixed, arrived)
    end_mixed, far, near = tie((end_mixed, far, near))
    far = exchange(far)
    end = exchange(end_products(end_mixed, fourth))

    def gather(part, start):
        where = jnp.arange(Y)[:, None, None] * SLOTS + start + jnp.arange(part.shape[2])
        where = jnp.broadcast_to(where, part.shape[:3])
        pick = (slot[0][:, None, None, None] == where).astype(jnp.bfloat16)
        return jnp.einsum("kyms,ymsil->kil", pick, part, preferred_element_type=jnp.float32)

    total = gather(near, 0) + gather(far, 5 * CAP) + gather(end, 7 * CAP)
    return total.astype(jnp.bfloat16)


def solution(mesh):
    fine = Mesh(mesh.devices.reshape(Z, Y, X, C), ("z", "y", "x", "c"))
    bond = ("z", "y")
    placed = (
        P(bond, None, None),
        P(("x", "c"), bond, None, None),
        P(("x", "c"), bond, None, None),
        P(bond),
    )
    return jax.shard_map(
        on_device, mesh=fine, in_specs=placed, out_specs=P(bond, ("x", "c"), None), check_vma=False
    )
```

```python
import functools

import jax
import jax.numpy as jnp
from jax import lax
from jax.experimental import pallas as pl
from jax.experimental.pallas import tpu as pltpu
from jax.sharding import Mesh, PartitionSpec as P

Z, Y, X, C = 8, 4, 4, 2
M = X * C
CAP = 3
SLOTS = Z * CAP
OFFSETS = (0, -1, 1, -2, 2, -3, 3, 4)
RANK = tuple(OFFSETS.index(((d + 3) % Z) - 3) for d in range(Z))
RIGHT = [(i, (i + 1) % Z) for i in range(Z)]
LEFT = [(i, (i - 1) % Z) for i in range(Z)]
UP = [(i, (i + 1) % Y) for i in range(Y)]
DOWN = [(i, (i - 1) % Y) for i in range(Y)]


def left_products(blocks, psi):
    terms, width = blocks.shape[0], blocks.shape[-1]
    mixed = jnp.dot(
        blocks.reshape(terms * width, width), psi, preferred_element_type=jnp.float32
    ).astype(jnp.bfloat16)
    return jnp.concatenate([mixed[w * width : (w + 1) * width] for w in range(terms)], axis=1)


def times_right(mixed, chosen):
    total = lax.dot_general(
        mixed,
        jnp.concatenate([chosen[w, 0] for w in range(chosen.shape[0])], axis=1),
        (((1,), (1,)), ((), ())),
        preferred_element_type=jnp.float32,
    )
    width = total.shape[0]
    return total.astype(jnp.bfloat16).reshape(M, width // M, width)


def left_products_turned(blocks, psi):
    terms, width = blocks.shape[0], blocks.shape[-1]
    mixed = jnp.dot(
        blocks.reshape(terms * width, width), psi, preferred_element_type=jnp.float32
    )
    turned = [mixed[w * width : (w + 1) * width].T for w in range(terms)]
    return jnp.concatenate(turned, axis=0).astype(jnp.bfloat16)


def right_times(chosen, turned):
    wide = jnp.concatenate([chosen[w, 0] for w in range(chosen.shape[0])], axis=1)
    total = jnp.dot(wide, turned, preferred_element_type=jnp.float32).T
    width = total.shape[0]
    return total.astype(jnp.bfloat16).reshape(M, width // M, width)


def middle_kernel(near, info_ref, low_psi, high_psi, *refs):
    own, above, low_far, high_far, below = refs[:5]
    rights = refs[5 : 5 + near]
    near_ref, far_ref, end_ref, left, right, left_sems, right_sems = refs[5 + near :]
    home = pl.program_id(0)
    owned = own.shape[1]
    far = far_ref.shape[1] // CAP

    def left_copy(source, sector, i):
        return pltpu.make_async_copy(source.at[:, pl.ds(sector, 1)], left.at[i], left_sems.at[i])

    def right_copy(source, sector, i):
        return pltpu.make_async_copy(source.at[:, pl.ds(sector, 1)], right.at[i], right_sems.at[i])

    def start_home(h, carry):
        apart = (h + Y - info_ref[Y * SLOTS]) % Y

        def start_lefts(pick):
            for q in range(SLOTS):
                pick(info_ref[h * SLOTS + q] // 16, h * SLOTS + q)

        def both_halves(sector, i):
            @pl.when(sector < owned // 2)
            def _():
                left_copy(low_far, sector, i).start()

            @pl.when(sector >= owned // 2)
            def _():
                left_copy(high_far, sector - owned // 2, i).start()

        for n, source in ((0, own), (1, above), (3, below)):

            @pl.when(apart == n)
            def _(source=source):
                start_lefts(lambda sector, i: left_copy(source, sector, i).start())

        @pl.when(apart == 2)
        def _():
            start_lefts(both_halves)

        for q in range(near * CAP):
            sector = info_ref[h * SLOTS + q] % 16
            right_copy(rights[q // CAP], sector, h * near * CAP + q).start()
        return carry

    @pl.when(home == 0)
    def _():
        lax.fori_loop(0, Y, start_home, 0)

    for q in range(SLOTS):
        left_copy(own, 0, home * SLOTS + q).wait()
    for q in range(near * CAP):
        right_copy(rights[0], 0, home * near * CAP + q).wait()
    half = SLOTS // C
    for q in range(SLOTS):
        psi = low_psi[0, q] if q < half else high_psi[0, q - half]
        blocks = left[home * SLOTS + q, :, 0]
        if q < near * CAP:
            chosen = right[home * near * CAP + q]
            near_ref[0, :, q] = times_right(left_products(blocks, psi), chosen)
        elif q < (near + far) * CAP:
            far_ref[0, q - near * CAP] = left_products_turned(blocks, psi)
        else:
            end_ref[0, q - (near + far) * CAP] = left_products_turned(blocks, psi)


def far_kernel(count, info_ref, mixed_ref, *refs):
    rights, (out_ref, held, sems) = refs[:count], refs[count:]
    copies = []
    for h in range(Y):
        for s in range(count * CAP):
            place = s // CAP
            sector = info_ref[h * SLOTS + (Z - 1 - count) * CAP + s] % 16
            copies.append(
                pltpu.make_async_copy(
                    rights[place].at[:, pl.ds(sector, 1)],
                    held.at[h * count * CAP + s],
                    sems.at[h * count * CAP + s],
                )
            )
    for copy in copies:
        copy.start()
    for h in range(Y):
        slots = range(h * count * CAP, (h + 1) * count * CAP)
        for i in slots:
            copies[i].wait()
        for s, i in enumerate(slots):
            out_ref[h, :, s] = right_times(held[i], mixed_ref[h, s])


def end_kernel(mixed_ref, low, high, out_ref):
    for h in range(Y):
        side, first = (low, h * CAP) if h < Y // 2 else (high, (h - Y // 2) * CAP)
        for s in range(CAP):
            chosen = side[:, first + s : first + s + 1]
            out_ref[h, :, s] = right_times(chosen, mixed_ref[h, s])


def fetch_kernel(low_index, high_index, low_ref, high_ref, low_out, high_out, sems):
    count = low_out.shape[1]
    copies = []
    for i in range(count):
        for n, (index, source, out) in enumerate(
            ((low_index, low_ref, low_out), (high_index, high_ref, high_out))
        ):
            copies.append(
                pltpu.make_async_copy(
                    source.at[:, pl.ds(index[i], 1)], out.at[:, pl.ds(i, 1)], sems.at[2 * i + n]
                )
            )
    for copy in copies:
        copy.start()
    for copy in copies:
        copy.wait()


PARAMS = pltpu.CompilerParams(vmem_limit_bytes=60 * 1024 * 1024)


def cost(slots, matmuls, terms, width):
    return pl.CostEstimate(
        flops=2 * slots * matmuls * terms * width**3,
        bytes_accessed=slots * (matmuls * terms + 2) * width * width * 2,
        transcendentals=0,
    )


def middle_products(info, psi, lefts, rights):
    terms, _, width, _ = lefts[0].shape
    near, far = len(rights), Z - 1 - len(rights)
    one = (terms, 1, width, width)
    turned = [
        jax.ShapeDtypeStruct((Y, n * CAP, terms * width, width), jnp.bfloat16) for n in (far, 1)
    ]
    out = jax.ShapeDtypeStruct((Y, M, near * CAP, width // M, width), jnp.bfloat16)
    per_home = lambda shape: pl.BlockSpec(
        (1,) + shape[1:], lambda h, info: (h,) + (0,) * (len(shape) - 1)
    )
    return pl.pallas_call(
        functools.partial(middle_kernel, near),
        out_shape=[out] + turned,
        grid_spec=pltpu.PrefetchScalarGridSpec(
            num_scalar_prefetch=1,
            grid=(Y,),
            in_specs=[per_home(p.shape) for p in psi]
            + [pl.BlockSpec(memory_space=pl.ANY)] * (len(lefts) + near),
            out_specs=[per_home(o.shape) for o in [out] + turned],
            scratch_shapes=[
                pltpu.VMEM((Y * SLOTS,) + one, jnp.bfloat16),
                pltpu.VMEM((Y * near * CAP,) + one, jnp.bfloat16),
                pltpu.SemaphoreType.DMA((Y * SLOTS,)),
                pltpu.SemaphoreType.DMA((Y * near * CAP,)),
            ],
        ),
        compiler_params=PARAMS,
        cost_estimate=cost(Y * SLOTS, 2, terms, width),
    )(info, *psi, *lefts, *rights)


SMALL = pltpu.CompilerParams(vmem_limit_bytes=24 * 1024 * 1024)
IN_VMEM = pl.BlockSpec(memory_space=pltpu.VMEM)
ANYWHERE = pl.BlockSpec(memory_space=pl.ANY)


def far_products(info, mixed, arrived):
    slots, width = mixed.shape[1], mixed.shape[3]
    terms = mixed.shape[2] // width
    return pl.pallas_call(
        functools.partial(far_kernel, len(arrived)),
        out_shape=jax.ShapeDtypeStruct((Y, M, slots, width // M, width), jnp.bfloat16),
        in_specs=[pl.BlockSpec(memory_space=pltpu.SMEM), IN_VMEM] + [ANYWHERE] * len(arrived),
        out_specs=IN_VMEM,
        scratch_shapes=[
            pltpu.VMEM((Y * slots, terms, 1, width, width), jnp.bfloat16),
            pltpu.SemaphoreType.DMA((Y * slots,)),
        ],
        compiler_params=SMALL,
        cost_estimate=cost(Y * slots, 2, terms, width),
    )(info, mixed, *arrived)


def end_products(mixed, sent):
    slots, width = mixed.shape[1], mixed.shape[3]
    return pl.pallas_call(
        end_kernel,
        out_shape=jax.ShapeDtypeStruct((Y, M, slots, width // M, width), jnp.bfloat16),
        in_specs=[IN_VMEM] * 3,
        out_specs=IN_VMEM,
        compiler_params=SMALL,
        cost_estimate=cost(Y * slots, 2, mixed.shape[2] // width, width),
    )(mixed, *sent)


def fetch(low, high, low_index, high_index):
    count = low_index.shape[0]
    out = jax.ShapeDtypeStruct((low.shape[0], count) + low.shape[2:], low.dtype)
    return pl.pallas_call(
        fetch_kernel,
        out_shape=[out, out],
        in_specs=[pl.BlockSpec(memory_space=pltpu.SMEM)] * 2 + [ANYWHERE] * 2,
        out_specs=[IN_VMEM] * 2,
        scratch_shapes=[pltpu.SemaphoreType.DMA((2 * count,))],
        compiler_params=SMALL,
        cost_estimate=pl.CostEstimate(
            flops=0, bytes_accessed=4 * out.size * 2, transcendentals=0
        ),
    )(low_index, high_index, low, high)


def exchange(part):
    part = part.reshape((Y * M,) + part.shape[2:])
    part = lax.all_to_all(part, ("y", "x", "c"), split_axis=0, concat_axis=0, tiled=True)
    return part.reshape((Y, M) + part.shape[1:])


def on_device(wavefunction, left_environment, right_environment, right_sector):
    z, y, core = (lax.axis_index(name) for name in ("z", "y", "c"))
    blocks, width = wavefunction.shape[:2]
    owned = left_environment.shape[1]
    members = blocks // owned
    tie = lax.optimization_barrier

    def step(moving, axis="z"):
        to_next, to_last = (RIGHT, LEFT) if axis == "z" else (UP, DOWN)
        return [lax.ppermute(moving[0], axis, to_next), lax.ppermute(moving[1], axis, to_last)]

    first = step([right_environment] * 2)

    index = jnp.arange(blocks, dtype=jnp.int32)
    earlier = index[None, :] < index[:, None]

    def slots_of(sectors, plane):
        owner = sectors // owned
        same = owner[:, :, None] == owner[:, None, :]
        place = jnp.sum((same & earlier).astype(jnp.int32), axis=2)
        offset = (owner // Y - plane) % Z
        rank = sum(jnp.where(offset == d, RANK[d], 0) for d in range(Z))
        return owner % Y, rank * CAP + place

    def into(slots, values, count):
        hit = slots[:, None, :] == jnp.arange(count, dtype=jnp.int32)[None, :, None]
        return jnp.sum(jnp.where(hit, values[:, None, :], 0), axis=2)

    column, slot = slots_of(right_sector[None], z)
    slot = column * SLOTS + slot
    split = SLOTS // C
    mine = (slot // SLOTS) * split + jnp.where((slot % SLOTS) // split == core, slot % split, -Y * SLOTS)
    source = into(mine, index[None], Y * split)[0]
    outgoing = wavefunction.at[source].get(mode="promise_in_bounds")
    outgoing = outgoing.reshape((Y, split) + wavefunction.shape[1:])

    sectors = jnp.broadcast_to(right_sector, (Y, blocks))
    sectors = lax.all_to_all(sectors, "y", split_axis=0, concat_axis=0, tiled=True)
    left_environment, sectors = tie((left_environment, sectors))
    near_left = step([left_environment] * 2, "y")
    column, here = slots_of(sectors, z)
    here = jnp.where(column == y, here, -1)
    info = into(here, (index // members) * 16 + sectors % owned, SLOTS)
    info = jnp.concatenate([info.reshape(-1), y[None].astype(jnp.int32)])

    last = info[: Y * SLOTS].reshape(Y, SLOTS)[:, SLOTS - CAP :] % owned
    wanted = [
        lax.ppermute(last[: Y // 2].reshape(-1), "z", LEFT),
        lax.ppermute(last[Y // 2 :].reshape(-1), "z", RIGHT),
    ]
    first, outgoing, wanted = tie((first, outgoing, wanted))
    psi = lax.all_to_all(outgoing, "y", split_axis=0, concat_axis=0, tiled=True)
    second = step(first)
    far_left = step([near_left[0][:, : owned // 2], near_left[1][:, owned // 2 :]], "y")
    other = lax.ppermute(psi, "c", [(0, 1), (1, 0)])
    psi = (jnp.where(core == 0, psi, other), jnp.where(core == 0, other, psi))
    second, psi, far_left = tie((second, psi, far_left))
    third = step(second)
    lefts = (left_environment, near_left[1], far_left[0], far_left[1], near_left[0])
    arrived = [right_environment] + first + second
    near, far_mixed, end_mixed = middle_products(info, psi, lefts, arrived)
    wanted, near, far_mixed, end_mixed = tie((wanted, near, far_mixed, end_mixed))
    fourth = step(fetch(*third, *wanted))
    near = exchange(near)
    far = far_products(info, far_mixed, third)
    end_mixed, far, near = tie((end_mixed, far, near))
    far = exchange(far)
    end = exchange(end_products(end_mixed, fourth))

    def gather(part, start):
        where = jnp.arange(Y)[:, None, None] * SLOTS + start + jnp.arange(part.shape[2])
        where = jnp.broadcast_to(where, part.shape[:3])
        pick = (slot[0][:, None, None, None] == where).astype(jnp.bfloat16)
        return jnp.einsum("kyms,ymsil->kil", pick, part, preferred_element_type=jnp.float32)

    total = gather(near, 0) + gather(far, 5 * CAP) + gather(end, 7 * CAP)
    return total.astype(jnp.bfloat16)


def solution(mesh):
    fine = Mesh(mesh.devices.reshape(Z, Y, X, C), ("z", "y", "x", "c"))
    bond = ("z", "y")
    placed = (
        P(bond, None, None),
        P(("x", "c"), bond, None, None),
        P(("x", "c"), bond, None, None),
        P(bond),
    )
    return jax.shard_map(
        on_device, mesh=fine, in_specs=placed, out_specs=P(bond, ("x", "c"), None), check_vma=False
    )
```

```python
import functools

import jax
import jax.numpy as jnp
from jax import lax
from jax.experimental import pallas as pl
from jax.experimental.pallas import tpu as pltpu
from jax.sharding import Mesh, PartitionSpec as P

Z, Y, X, C = 8, 4, 4, 2
M = X * C
CAP = 3
SLOTS = Z * CAP
OFFSETS = (0, -1, 1, -2, 2, -3, 3, 4)
RANK = tuple(OFFSETS.index(((d + 3) % Z) - 3) for d in range(Z))
TILE = 16
MIRROR = tuple(OFFSETS.index(-d if -d in OFFSETS else d) for d in OFFSETS)
PSI_ORDER = (0, 1, 2, 7, 3, 4, 5, 6)


def ring(size, way):
    return [
        (i * C + c, (i + (way if c == 0 else -way)) % size * C + c)
        for i in range(size)
        for c in range(C)
    ]


def left_products(blocks, psi):
    terms, width = blocks.shape[0], blocks.shape[-1]
    mixed = jnp.dot(
        blocks.reshape(terms * width, width), psi, preferred_element_type=jnp.float32
    ).astype(jnp.bfloat16)
    return jnp.concatenate([mixed[w * width : (w + 1) * width] for w in range(terms)], axis=1)


def times_right(mixed, chosen):
    total = lax.dot_general(
        mixed,
        jnp.concatenate([chosen[w, 0] for w in range(chosen.shape[0])], axis=1),
        (((1,), (1,)), ((), ())),
        preferred_element_type=jnp.float32,
    )
    width = total.shape[0]
    return total.astype(jnp.bfloat16).reshape(M, width // M, width)


def left_products_turned(blocks, psi):
    terms, width = blocks.shape[0], blocks.shape[-1]
    mixed = jnp.dot(
        blocks.reshape(terms * width, width), psi, preferred_element_type=jnp.float32
    )
    turned = [mixed[w * width : (w + 1) * width].T for w in range(terms)]
    return jnp.concatenate(turned, axis=0).astype(jnp.bfloat16)


def right_times(chosen, turned):
    wide = jnp.concatenate([chosen[w, 0] for w in range(chosen.shape[0])], axis=1)
    total = jnp.dot(wide, turned, preferred_element_type=jnp.float32).T
    width = total.shape[0]
    return total.astype(jnp.bfloat16).reshape(M, width // M, width)


def middle_kernel(near, info_ref, *refs):
    psi, lefts, rights = refs[:C], refs[C : C + Y], refs[C + Y : C + Y + near]
    near_ref, far_ref, low_ref, high_ref, left, right, left_sems, right_sems = refs[C + Y + near :]
    home = pl.program_id(0)
    far = far_ref.shape[1] // CAP

    def left_copy(source, sector, i):
        return pltpu.make_async_copy(source.at[:, pl.ds(sector, 1)], left.at[i], left_sems.at[i])

    def right_copy(source, sector, i):
        return pltpu.make_async_copy(source.at[:, pl.ds(sector, 1)], right.at[i], right_sems.at[i])

    def start_home(h, carry):
        apart = (Y + info_ref[Y * SLOTS + 1] * (h - info_ref[Y * SLOTS])) % Y
        for n, source in enumerate(lefts):

            @pl.when(apart == n)
            def _(source=source):
                for q in range(SLOTS):
                    left_copy(source, info_ref[h * SLOTS + q] // 16, h * SLOTS + q).start()

        for q in range(near * CAP):
            sector = info_ref[h * SLOTS + q] % 16
            right_copy(rights[q // CAP], sector, h * near * CAP + q).start()
        return carry

    @pl.when(home == 0)
    def _():
        lax.fori_loop(0, Y, start_home, 0)

    for q in range(SLOTS):
        left_copy(lefts[0], 0, home * SLOTS + q).wait()
    for q in range(near * CAP):
        right_copy(rights[0], 0, home * near * CAP + q).wait()
    half = Z // C
    flipped = (1 - info_ref[Y * SLOTS + 1]) // 2
    for q in range(SLOTS):
        p, c = divmod(q, CAP)
        part, at = divmod(PSI_ORDER.index(p), half)
        shift = PSI_ORDER.index(MIRROR[p]) % half - at
        blocks = left[home * SLOTS + q, :, 0]
        mine = psi[part][0, at * CAP + c + flipped * (shift * CAP)]
        if q < near * CAP:
            chosen = right[home * near * CAP + q]
            to = q + flipped * ((MIRROR[p] - p) * CAP)
            near_ref[0, :, pl.ds(to, 1)] = times_right(left_products(blocks, mine), chosen)[:, None]
        elif q < (near + far) * CAP:
            far_ref[0, q - near * CAP] = left_products_turned(blocks, mine)
        else:
            turned = left_products_turned(blocks, mine)
            sector = info_ref[home * SLOTS + q] % 16
            tile = jnp.full((TILE, turned.shape[1]), sector, jnp.int32).astype(jnp.float32)
            turned = jnp.concatenate([turned, tile.astype(jnp.bfloat16)], axis=0)

            @pl.when(home < Y // 2)
            def _(turned=turned, i=q - (near + far) * CAP):
                low_ref[0, i] = turned

            @pl.when(home >= Y // 2)
            def _(turned=turned, i=q - (near + far) * CAP):
                high_ref[0, i] = turned


def far_kernel(count, info_ref, mixed_ref, *refs):
    rights, (out_ref, held, held_mixed, sems, mixed_sems) = refs[:count], refs[count:]
    flipped = (1 - info_ref[Y * SLOTS + 1]) // 2
    copies = []
    mixed_copies = [
        pltpu.make_async_copy(mixed_ref.at[h], held_mixed.at[h], mixed_sems.at[h])
        for h in range(Y)
    ]
    for h in range(Y):
        for s in range(count * CAP):
            place = s // CAP
            sector = info_ref[h * SLOTS + (Z - 1 - count) * CAP + s] % 16
            copies.append(
                pltpu.make_async_copy(
                    rights[place].at[:, pl.ds(sector, 1)],
                    held.at[h * count * CAP + s],
                    sems.at[h * count * CAP + s],
                )
            )
    for h in range(Y):
        mixed_copies[h].start()
        for copy in copies[h * count * CAP : (h + 1) * count * CAP]:
            copy.start()
    for h in range(Y):
        slots = range(h * count * CAP, (h + 1) * count * CAP)
        mixed_copies[h].wait()
        for i in slots:
            copies[i].wait()
        for s, i in enumerate(slots):
            to = s + flipped * (CAP if s < CAP else -CAP)
            out_ref[h, :, pl.ds(to, 1)] = right_times(held[i], held_mixed[h, s])[:, None]


def guest_kernel(
    info_ref, low_index, high_index, low_ref, high_ref, one_ref, other_ref,
    out_ref, held, guests, sems, guest_sems,
):
    half = Y // 2 * CAP
    rows = low_ref.shape[2] - TILE
    sides = [
        pltpu.make_async_copy(side, guests.at[pl.ds(n * (Y // 2), Y // 2)], guest_sems.at[n])
        for n, side in enumerate((low_ref, high_ref))
    ]
    for side in sides:
        side.start()

    def start(low_source, high_source):
        for i in range(Y * CAP):
            source = low_source if i < half else high_source
            index = low_index if i < half else high_index
            sector = index[i % half // CAP, i % CAP]
            pltpu.make_async_copy(
                source.at[:, pl.ds(sector, 1)], held.at[i], sems.at[i]
            ).start()

    @pl.when(info_ref[Y * SLOTS + 1] == 1)
    def _():
        start(other_ref, one_ref)

    @pl.when(info_ref[Y * SLOTS + 1] != 1)
    def _():
        start(one_ref, other_ref)

    for h in range(Y):
        if h % (Y // 2) == 0:
            sides[h // (Y // 2)].wait()
        slots = range(h * CAP, (h + 1) * CAP)
        for i in slots:
            pltpu.make_async_copy(one_ref.at[:, pl.ds(0, 1)], held.at[i], sems.at[i]).wait()
        for s, i in enumerate(slots):
            out_ref[h, :, s] = right_times(held[i], guests[h, s, :rows])


LARGE = pltpu.CompilerParams(vmem_limit_bytes=60 * 1024 * 1024)


def cost(slots, matmuls, terms, width):
    return pl.CostEstimate(
        flops=2 * slots * matmuls * terms * width**3,
        bytes_accessed=slots * (matmuls * terms + 2) * width * width * 2,
        transcendentals=0,
    )


def middle_products(info, psi, lefts, rights):
    terms, _, width, _ = lefts[0].shape
    near, far = len(rights), Z - 1 - len(rights)
    one = (terms, 1, width, width)
    turned = jax.ShapeDtypeStruct((Y, far * CAP, terms * width, width), jnp.bfloat16)
    guest = jax.ShapeDtypeStruct((Y // 2, CAP, terms * width + TILE, width), jnp.bfloat16)
    out = jax.ShapeDtypeStruct((Y, M, near * CAP, width // M, width), jnp.bfloat16)
    per_home = lambda shape: pl.BlockSpec(
        (1,) + shape[1:], lambda h, info: (h,) + (0,) * (len(shape) - 1)
    )
    return pl.pallas_call(
        functools.partial(middle_kernel, near),
        out_shape=[out, turned, guest, guest],
        grid_spec=pltpu.PrefetchScalarGridSpec(
            num_scalar_prefetch=1,
            grid=(Y,),
            in_specs=[per_home(p.shape) for p in psi]
            + [pl.BlockSpec(memory_space=pl.ANY)] * (len(lefts) + near),
            out_specs=[
                per_home(out.shape),
                per_home(turned.shape),
                pl.BlockSpec(
                    (1,) + guest.shape[1:],
                    lambda h, info: (jnp.minimum(h, Y // 2 - 1), 0, 0, 0),
                ),
                pl.BlockSpec(
                    (1,) + guest.shape[1:],
                    lambda h, info: (jnp.maximum(h - Y // 2, 0), 0, 0, 0),
                ),
            ],
            scratch_shapes=[
                pltpu.VMEM((Y * SLOTS,) + one, jnp.bfloat16),
                pltpu.VMEM((Y * near * CAP,) + one, jnp.bfloat16),
                pltpu.SemaphoreType.DMA((Y * SLOTS,)),
                pltpu.SemaphoreType.DMA((Y * near * CAP,)),
            ],
        ),
        compiler_params=LARGE,
        cost_estimate=cost(Y * SLOTS, 2, terms, width),
    )(info, *psi, *lefts, *rights)


SMALL = pltpu.CompilerParams(vmem_limit_bytes=24 * 1024 * 1024)
IN_VMEM = pl.BlockSpec(memory_space=pltpu.VMEM)
IN_HBM = pl.BlockSpec(memory_space=pltpu.HBM)


def far_products(info, mixed, arrived):
    slots, width = mixed.shape[1], mixed.shape[3]
    terms = mixed.shape[2] // width
    return pl.pallas_call(
        functools.partial(far_kernel, len(arrived)),
        out_shape=jax.ShapeDtypeStruct((Y, M, slots, width // M, width), jnp.bfloat16),
        in_specs=[pl.BlockSpec(memory_space=pltpu.SMEM)] + [IN_HBM] * (1 + len(arrived)),
        out_specs=IN_VMEM,
        scratch_shapes=[
            pltpu.VMEM((Y * slots, terms, 1, width, width), jnp.bfloat16),
            pltpu.VMEM(mixed.shape, jnp.bfloat16),
            pltpu.SemaphoreType.DMA((Y * slots,)),
            pltpu.SemaphoreType.DMA((Y,)),
        ],
        compiler_params=LARGE,
        cost_estimate=cost(Y * slots, 2, terms, width),
    )(info, mixed, *arrived)


def guest_products(info, low_index, high_index, low, high, arrived):
    terms, _, width, _ = arrived[0].shape
    return pl.pallas_call(
        guest_kernel,
        out_shape=jax.ShapeDtypeStruct((Y, M, CAP, width // M, width), jnp.bfloat16),
        in_specs=[pl.BlockSpec(memory_space=pltpu.SMEM)] * 3 + [IN_HBM] * 4,
        out_specs=IN_VMEM,
        scratch_shapes=[
            pltpu.VMEM((Y * CAP, terms, 1, width, width), jnp.bfloat16),
            pltpu.VMEM((Y,) + low.shape[1:], jnp.bfloat16),
            pltpu.SemaphoreType.DMA((Y * CAP,)),
            pltpu.SemaphoreType.DMA((2,)),
        ],
        compiler_params=LARGE,
        cost_estimate=cost(Y * CAP, 2, terms, width),
    )(info, low_index, high_index, low, high, *arrived)


def settle_kernel(place_ref, *refs):
    parts, out_ref = refs[:-1], refs[-1]
    starts = [0]
    for part in parts:
        starts.append(starts[-1] + part.shape[0])
    for k in range(out_ref.shape[0]):
        place = place_ref[k]
        for n, part in enumerate(parts):

            @pl.when((place >= starts[n]) & (place < starts[n + 1]))
            def _(k=k, part=part, start=starts[n], place=place):
                out_ref[k] = part[place - start]


def settle(place, parts):
    return pl.pallas_call(
        settle_kernel,
        out_shape=jax.ShapeDtypeStruct(place.shape + parts[0].shape[1:], parts[0].dtype),
        in_specs=[pl.BlockSpec(memory_space=pltpu.SMEM)] + [IN_VMEM] * len(parts),
        out_specs=IN_VMEM,
        compiler_params=SMALL,
    )(place, *parts)


def exchange(part):
    part = part.reshape((Y * M,) + part.shape[2:])
    part = lax.all_to_all(part, ("y", "x", "c"), split_axis=0, concat_axis=0, tiled=True)
    return part.reshape((Y, M) + part.shape[1:])


def add_up(part):
    return part.astype(jnp.float32).sum(axis=1).astype(jnp.bfloat16)


def on_device(wavefunction, left_environment, right_environment, right_sector):
    z, y, core = (lax.axis_index(name) for name in ("z", "y", "c"))
    blocks, width = wavefunction.shape[:2]
    owned = left_environment.shape[1]
    members = blocks // owned
    tie = lax.optimization_barrier

    way = 1 - 2 * core

    def hop(moved, axis, direction):
        size = Z if axis == "z" else Y
        return lax.ppermute(moved, (axis, "c"), ring(size, direction))

    def step(moving, axis="z"):
        return [hop(moving[0], axis, 1), hop(moving[1], axis, -1)]

    first = step([right_environment] * 2)

    index = jnp.arange(blocks, dtype=jnp.int32)
    earlier = index[None, :] < index[:, None]

    def slots_of(sectors, direction):
        owner = sectors // owned
        same = owner[:, :, None] == owner[:, None, :]
        place = jnp.sum((same & earlier).astype(jnp.int32), axis=2)
        offset = (direction * (owner // Y - z)) % Z
        rank = sum(jnp.where(offset == d, RANK[d], 0) for d in range(Z))
        return owner % Y, rank * CAP + place

    def into(slots, values, count):
        hit = slots[:, None, :] == jnp.arange(count, dtype=jnp.int32)[None, :, None]
        return jnp.sum(jnp.where(hit, values[:, None, :], 0), axis=2)

    column, slot = slots_of(right_sector[None], 1)
    slot = column * SLOTS + slot
    split = SLOTS // C
    rank = (slot % SLOTS) // CAP
    position = sum(jnp.where(rank == p, n, 0) for n, p in enumerate(PSI_ORDER)) * CAP + slot % CAP
    mine = column * split + jnp.where(position // split == core, position % split, -Y * SLOTS)
    source = into(mine, index[None], Y * split)[0]
    outgoing = wavefunction.at[source].get(mode="promise_in_bounds")
    outgoing = outgoing.reshape((Y, split) + wavefunction.shape[1:])

    sectors = jnp.broadcast_to(right_sector, (Y, blocks))
    sectors = lax.all_to_all(sectors, "y", split_axis=0, concat_axis=0, tiled=True)
    left_environment, sectors = tie((left_environment, sectors))
    near_left = step([left_environment] * 2, "y")
    column, here = slots_of(sectors, way)
    here = jnp.where(column == y, here, -1)
    info = into(here, (index // members) * 16 + sectors % owned, SLOTS)
    info = jnp.concatenate([info.reshape(-1), jnp.stack([y, way]).astype(jnp.int32)])

    second = step(first)
    psi = lax.all_to_all(outgoing, "y", split_axis=0, concat_axis=0, tiled=True)
    far_left = hop(near_left[0], "y", 1)
    other = lax.ppermute(psi, "c", [(0, 1), (1, 0)])
    psi = (jnp.where(core == 0, psi, other), jnp.where(core == 0, other, psi))
    second, psi = tie((second, psi))
    third = step(second)
    lefts = (left_environment, near_left[1], far_left, near_left[0])
    arrived = [right_environment] + first + second
    near, far_mixed, low, high = middle_products(info, psi, lefts, arrived)
    low = lax.ppermute(low, "z", [(i, (i + 1) % Z) for i in range(Z)])
    high = lax.ppermute(high, "z", [(i, (i - 1) % Z) for i in range(Z)])
    far = far_products(info, far_mixed, third)
    far, near = tie((far, exchange(near)))
    sectors = [g[:, :, -1, 0].astype(jnp.int32) for g in (low, high)]
    guests = guest_products(info, *sectors, low, high, third)
    guests, far = tie((guests, exchange(far)))
    guests = add_up(exchange(guests))
    flat = lambda part: part.reshape((-1,) + part.shape[2:])
    column, at = slot[0] // SLOTS, slot[0] % SLOTS
    first_far, first_end = 5 * CAP, 7 * CAP
    near, far = flat(add_up(near)), flat(add_up(far))
    place = jnp.where(
        at < first_far,
        column * first_far + at,
        near.shape[0] + column * (first_end - first_far) + at - first_far,
    )
    settled = settle(jnp.where(at < first_end, place, -1), (near, far))
    guests, settled = tie((guests, settled))
    home = [
        (i * Y + j, (i + (-1 if j < Y // 2 else 1)) % Z * Y + j) for i in range(Z) for j in range(Y)
    ]
    end = lax.ppermute(guests, ("z", "y"), home)

    end = flat(end)
    place = jnp.where(at < first_end, end.shape[0] + index, column * CAP + at - first_end)
    return settle(place, (end, settled))


def solution(mesh):
    fine = Mesh(mesh.devices.reshape(Z, Y, X, C), ("z", "y", "x", "c"))
    bond = ("z", "y")
    placed = (
        P(bond, None, None),
        P(("x", "c"), bond, None, None),
        P(("x", "c"), bond, None, None),
        P(bond),
    )
    return jax.shard_map(
        on_device, mesh=fine, in_specs=placed, out_specs=P(bond, ("x", "c"), None), check_vma=False
    )
```

```python
import functools

import jax
import jax.numpy as jnp
from jax import lax
from jax.experimental import pallas as pl
from jax.experimental.pallas import tpu as pltpu
from jax.sharding import Mesh, PartitionSpec as P

Z, Y, X, C = 8, 4, 4, 2
M = X * C
CAP = 3
SLOTS = Z * CAP
OFFSETS = (0, -1, 1, -2, 2, -3, 3, 4)
RANK = tuple(OFFSETS.index(((d + 3) % Z) - 3) for d in range(Z))
TILE = 16
MIRROR = tuple(OFFSETS.index(-d if -d in OFFSETS else d) for d in OFFSETS)
PSI_ORDER = (0, 1, 2, 7, 3, 4, 5, 6)


def ring(size, way):
    return [
        (i * C + c, (i + (way if c == 0 else -way)) % size * C + c)
        for i in range(size)
        for c in range(C)
    ]


def left_products(blocks, psi):
    terms, width = blocks.shape[0], blocks.shape[-1]
    mixed = jnp.dot(
        blocks.reshape(terms * width, width), psi, preferred_element_type=jnp.float32
    ).astype(jnp.bfloat16)
    return jnp.concatenate([mixed[w * width : (w + 1) * width] for w in range(terms)], axis=1)


def times_right(mixed, chosen):
    total = lax.dot_general(
        mixed,
        jnp.concatenate([chosen[w, 0] for w in range(chosen.shape[0])], axis=1),
        (((1,), (1,)), ((), ())),
        preferred_element_type=jnp.float32,
    )
    width = total.shape[0]
    return total.astype(jnp.bfloat16).reshape(M, width // M, width)


def left_products_turned(blocks, psi):
    terms, width = blocks.shape[0], blocks.shape[-1]
    mixed = jnp.dot(
        blocks.reshape(terms * width, width), psi, preferred_element_type=jnp.float32
    )
    turned = [mixed[w * width : (w + 1) * width].T for w in range(terms)]
    return jnp.concatenate(turned, axis=0).astype(jnp.bfloat16)


def right_times(chosen, turned):
    wide = jnp.concatenate([chosen[w, 0] for w in range(chosen.shape[0])], axis=1)
    total = jnp.dot(wide, turned, preferred_element_type=jnp.float32).astype(jnp.bfloat16).T
    width = total.shape[0]
    return total.reshape(M, width // M, width)


def middle_kernel(near, info_ref, *refs):
    psi, lefts, rights = refs[:C], refs[C : C + Y], refs[C + Y : C + Y + near]
    near_ref, far_ref, low_ref, high_ref, left, right, left_sems, right_sems = refs[C + Y + near :]
    home = pl.program_id(0)
    far = far_ref.shape[1] // CAP

    def left_copy(source, sector, i):
        return pltpu.make_async_copy(source.at[:, pl.ds(sector, 1)], left.at[i], left_sems.at[i])

    def right_copy(source, sector, i):
        return pltpu.make_async_copy(source.at[:, pl.ds(sector, 1)], right.at[i], right_sems.at[i])

    def start_home(h, carry):
        apart = (Y + info_ref[Y * SLOTS + 1] * (h - info_ref[Y * SLOTS])) % Y
        for n, source in enumerate(lefts):

            @pl.when(apart == n)
            def _(source=source):
                for q in range(SLOTS):
                    left_copy(source, info_ref[h * SLOTS + q] // 16, h * SLOTS + q).start()

        for q in range(near * CAP):
            sector = info_ref[h * SLOTS + q] % 16
            right_copy(rights[q // CAP], sector, h * near * CAP + q).start()
        return carry

    @pl.when(home == 0)
    def _():
        lax.fori_loop(0, Y, start_home, 0)

    for q in range(SLOTS):
        left_copy(lefts[0], 0, home * SLOTS + q).wait()
    for q in range(near * CAP):
        right_copy(rights[0], 0, home * near * CAP + q).wait()
    half = Z // C
    flipped = (1 - info_ref[Y * SLOTS + 1]) // 2
    for q in range(SLOTS):
        p, c = divmod(q, CAP)
        part, at = divmod(PSI_ORDER.index(p), half)
        shift = PSI_ORDER.index(MIRROR[p]) % half - at
        blocks = left[home * SLOTS + q, :, 0]
        mine = psi[part][0, at * CAP + c + flipped * (shift * CAP)]
        if q < near * CAP:
            chosen = right[home * near * CAP + q]
            to = q + flipped * ((MIRROR[p] - p) * CAP)
            near_ref[0, :, pl.ds(to, 1)] = times_right(left_products(blocks, mine), chosen)[:, None]
        elif q < (near + far) * CAP:
            far_ref[0, q - near * CAP] = left_products_turned(blocks, mine)
        else:
            turned = left_products_turned(blocks, mine)
            sector = info_ref[home * SLOTS + q] % 16
            tile = jnp.full((TILE, turned.shape[1]), sector, jnp.int32).astype(jnp.float32)
            turned = jnp.concatenate([turned, tile.astype(jnp.bfloat16)], axis=0)

            @pl.when(home < Y // 2)
            def _(turned=turned, i=q - (near + far) * CAP):
                low_ref[0, i] = turned

            @pl.when(home >= Y // 2)
            def _(turned=turned, i=q - (near + far) * CAP):
                high_ref[0, i] = turned


def far_kernel(count, info_ref, mixed_ref, *refs):
    rights, (out_ref, held, held_mixed, sems, mixed_sems) = refs[:count], refs[count:]
    flipped = (1 - info_ref[Y * SLOTS + 1]) // 2
    copies = []
    mixed_copies = [
        pltpu.make_async_copy(mixed_ref.at[h], held_mixed.at[h], mixed_sems.at[h])
        for h in range(Y)
    ]
    for h in range(Y):
        for s in range(count * CAP):
            place = s // CAP
            sector = info_ref[h * SLOTS + (Z - 1 - count) * CAP + s] % 16
            copies.append(
                pltpu.make_async_copy(
                    rights[place].at[:, pl.ds(sector, 1)],
                    held.at[h * count * CAP + s],
                    sems.at[h * count * CAP + s],
                )
            )
    for h in range(Y):
        mixed_copies[h].start()
        for copy in copies[h * count * CAP : (h + 1) * count * CAP]:
            copy.start()
    for h in range(Y):
        slots = range(h * count * CAP, (h + 1) * count * CAP)
        mixed_copies[h].wait()
        for i in slots:
            copies[i].wait()
        for s, i in enumerate(slots):
            to = s + flipped * (CAP if s < CAP else -CAP)
            out_ref[h, :, pl.ds(to, 1)] = right_times(held[i], held_mixed[h, s])[:, None]


def guest_kernel(index_ref, low_ref, high_ref, one_ref, other_ref, out_ref, held, sems):
    half = Y // 2 * CAP
    rows = low_ref.shape[2] - TILE

    def start(low_source, high_source):
        for i in range(Y * CAP):
            source = low_source if i < half else high_source
            pltpu.make_async_copy(
                source.at[:, pl.ds(index_ref[i], 1)], held.at[i], sems.at[i]
            ).start()

    @pl.when(index_ref[Y * CAP] == 1)
    def _():
        start(other_ref, one_ref)

    @pl.when(index_ref[Y * CAP] != 1)
    def _():
        start(one_ref, other_ref)

    for i in range(Y * CAP):
        pltpu.make_async_copy(one_ref.at[:, pl.ds(0, 1)], held.at[i], sems.at[i]).wait()
    for h in range(Y):
        guests = low_ref if h < Y // 2 else high_ref
        for s in range(CAP):
            mixed = guests[h % (Y // 2), s, :rows]
            out_ref[h, :, s] = right_times(held[h * CAP + s], mixed)


MIDDLE = pltpu.CompilerParams(vmem_limit_bytes=56 * 1024 * 1024)
LARGE = pltpu.CompilerParams(vmem_limit_bytes=60 * 1024 * 1024)


def cost(slots, matmuls, terms, width):
    return pl.CostEstimate(
        flops=2 * slots * matmuls * terms * width**3,
        bytes_accessed=slots * (matmuls * terms + 2) * width * width * 2,
        transcendentals=0,
    )


def middle_products(info, psi, lefts, rights):
    terms, _, width, _ = lefts[0].shape
    near, far = len(rights), Z - 1 - len(rights)
    one = (terms, 1, width, width)
    turned = jax.ShapeDtypeStruct((Y, far * CAP, terms * width, width), jnp.bfloat16)
    guest = jax.ShapeDtypeStruct((Y // 2, CAP, terms * width + TILE, width), jnp.bfloat16)
    out = jax.ShapeDtypeStruct((Y, M, near * CAP, width // M, width), jnp.bfloat16)
    per_home = lambda shape: pl.BlockSpec(
        (1,) + shape[1:], lambda h, info: (h,) + (0,) * (len(shape) - 1)
    )
    return pl.pallas_call(
        functools.partial(middle_kernel, near),
        out_shape=[out, turned, guest, guest],
        grid_spec=pltpu.PrefetchScalarGridSpec(
            num_scalar_prefetch=1,
            grid=(Y,),
            in_specs=[per_home(p.shape) for p in psi]
            + [pl.BlockSpec(memory_space=pl.ANY)] * (len(lefts) + near),
            out_specs=[
                per_home(out.shape),
                per_home(turned.shape),
                pl.BlockSpec(
                    (1,) + guest.shape[1:],
                    lambda h, info: (jnp.minimum(h, Y // 2 - 1), 0, 0, 0),
                ),
                pl.BlockSpec(
                    (1,) + guest.shape[1:],
                    lambda h, info: (jnp.maximum(h - Y // 2, 0), 0, 0, 0),
                ),
            ],
            scratch_shapes=[
                pltpu.VMEM((Y * SLOTS,) + one, jnp.bfloat16),
                pltpu.VMEM((Y * near * CAP,) + one, jnp.bfloat16),
                pltpu.SemaphoreType.DMA((Y * SLOTS,)),
                pltpu.SemaphoreType.DMA((Y * near * CAP,)),
            ],
        ),
        compiler_params=LARGE,
        cost_estimate=cost(Y * SLOTS, 2, terms, width),
    )(info, *psi, *lefts, *rights)


SMALL = pltpu.CompilerParams(vmem_limit_bytes=24 * 1024 * 1024)
IN_VMEM = pl.BlockSpec(memory_space=pltpu.VMEM)
IN_HBM = pl.BlockSpec(memory_space=pltpu.HBM)


def far_products(info, mixed, arrived):
    slots, width = mixed.shape[1], mixed.shape[3]
    terms = mixed.shape[2] // width
    return pl.pallas_call(
        functools.partial(far_kernel, len(arrived)),
        out_shape=jax.ShapeDtypeStruct((Y, M, slots, width // M, width), jnp.bfloat16),
        in_specs=[pl.BlockSpec(memory_space=pltpu.SMEM)] + [IN_HBM] * (1 + len(arrived)),
        out_specs=IN_VMEM,
        scratch_shapes=[
            pltpu.VMEM((Y * slots, terms, 1, width, width), jnp.bfloat16),
            pltpu.VMEM(mixed.shape, jnp.bfloat16),
            pltpu.SemaphoreType.DMA((Y * slots,)),
            pltpu.SemaphoreType.DMA((Y,)),
        ],
        compiler_params=MIDDLE,
        cost_estimate=cost(Y * slots, 2, terms, width),
    )(info, mixed, *arrived)


def guest_products(index, low, high, arrived):
    terms, _, width, _ = arrived[0].shape
    return pl.pallas_call(
        guest_kernel,
        out_shape=jax.ShapeDtypeStruct((Y, M, CAP, width // M, width), jnp.bfloat16),
        in_specs=[pl.BlockSpec(memory_space=pltpu.SMEM), IN_VMEM, IN_VMEM] + [IN_HBM] * 2,
        out_specs=IN_VMEM,
        scratch_shapes=[
            pltpu.VMEM((Y * CAP, terms, 1, width, width), jnp.bfloat16),
            pltpu.SemaphoreType.DMA((Y * CAP,)),
        ],
        compiler_params=SMALL,
        cost_estimate=cost(Y * CAP, 2, terms, width),
    )(index, low, high, *arrived)


def settle_kernel(place_ref, *refs):
    parts, out_ref = refs[:-1], refs[-1]
    starts = [0]
    for part in parts:
        starts.append(starts[-1] + part.shape[0])
    for k in range(out_ref.shape[0]):
        place = place_ref[k]
        for n, part in enumerate(parts):

            @pl.when((place >= starts[n]) & (place < starts[n + 1]))
            def _(k=k, part=part, start=starts[n], place=place):
                out_ref[k] = part[place - start]


def settle(place, parts):
    return pl.pallas_call(
        settle_kernel,
        out_shape=jax.ShapeDtypeStruct(place.shape + parts[0].shape[1:], parts[0].dtype),
        in_specs=[pl.BlockSpec(memory_space=pltpu.SMEM)] + [IN_VMEM] * len(parts),
        out_specs=IN_VMEM,
        compiler_params=SMALL,
    )(place, *parts)


def finish_kernel(target_ref, end_ref, settled_ref, out_ref, sems):
    del settled_ref
    copies = [
        pltpu.make_async_copy(end_ref.at[i], out_ref.at[target_ref[i]], sems.at[i])
        for i in range(end_ref.shape[0])
    ]
    for i, copy in enumerate(copies):
        pl.when(target_ref[i] >= 0)(copy.start)
    for i, copy in enumerate(copies):
        pl.when(target_ref[i] >= 0)(copy.wait)


def finish(target, end, settled):
    return pl.pallas_call(
        finish_kernel,
        out_shape=jax.ShapeDtypeStruct(settled.shape, settled.dtype),
        in_specs=[pl.BlockSpec(memory_space=pltpu.SMEM), IN_VMEM, IN_HBM],
        out_specs=IN_HBM,
        scratch_shapes=[pltpu.SemaphoreType.DMA(target.shape)],
        input_output_aliases={2: 0},
        compiler_params=SMALL,
    )(target, end, settled)


def exchange(part):
    part = part.reshape((Y * M,) + part.shape[2:])
    part = lax.all_to_all(part, ("y", "x", "c"), split_axis=0, concat_axis=0, tiled=True)
    return part.reshape((Y, M) + part.shape[1:])


def add_up(part):
    return part.astype(jnp.float32).sum(axis=1).astype(jnp.bfloat16)


def on_device(wavefunction, left_environment, right_environment, right_sector):
    z, y, core = (lax.axis_index(name) for name in ("z", "y", "c"))
    blocks, width = wavefunction.shape[:2]
    owned = left_environment.shape[1]
    members = blocks // owned
    tie = lax.optimization_barrier

    way = 1 - 2 * core

    def hop(moved, axis, direction):
        size = Z if axis == "z" else Y
        return lax.ppermute(moved, (axis, "c"), ring(size, direction))

    def step(moving, axis="z"):
        return [hop(moving[0], axis, 1), hop(moving[1], axis, -1)]

    first = step([right_environment] * 2)

    index = jnp.arange(blocks, dtype=jnp.int32)
    earlier = index[None, :] < index[:, None]

    def slots_of(sectors, direction):
        owner = sectors // owned
        same = owner[:, :, None] == owner[:, None, :]
        place = jnp.sum((same & earlier).astype(jnp.int32), axis=2)
        offset = (direction * (owner // Y - z)) % Z
        rank = sum(jnp.where(offset == d, RANK[d], 0) for d in range(Z))
        return owner % Y, rank * CAP + place

    def into(slots, values, count):
        hit = slots[:, None, :] == jnp.arange(count, dtype=jnp.int32)[None, :, None]
        return jnp.sum(jnp.where(hit, values[:, None, :], 0), axis=2)

    column, slot = slots_of(right_sector[None], 1)
    slot = column * SLOTS + slot
    split = SLOTS // C
    rank = (slot % SLOTS) // CAP
    position = sum(jnp.where(rank == p, n, 0) for n, p in enumerate(PSI_ORDER)) * CAP + slot % CAP
    mine = column * split + jnp.where(position // split == core, position % split, -Y * SLOTS)
    source = into(mine, index[None], Y * split)[0]
    outgoing = wavefunction.at[source].get(mode="promise_in_bounds")
    outgoing = outgoing.reshape((Y, split) + wavefunction.shape[1:])

    sectors = jnp.broadcast_to(right_sector, (Y, blocks))
    sectors = lax.all_to_all(sectors, "y", split_axis=0, concat_axis=0, tiled=True)
    left_environment, sectors = tie((left_environment, sectors))
    near_left = step([left_environment] * 2, "y")
    column, here = slots_of(sectors, way)
    here = jnp.where(column == y, here, -1)
    info = into(here, (index // members) * 16 + sectors % owned, SLOTS)
    info = jnp.concatenate([info.reshape(-1), jnp.stack([y, way]).astype(jnp.int32)])

    second = step(first)
    psi = lax.all_to_all(outgoing, "y", split_axis=0, concat_axis=0, tiled=True)
    far_left = hop(near_left[0], "y", 1)
    other = lax.ppermute(psi, "c", [(0, 1), (1, 0)])
    psi = (jnp.where(core == 0, psi, other), jnp.where(core == 0, other, psi))
    second, psi = tie((second, psi))
    third = step(second)
    lefts = (left_environment, near_left[1], far_left, near_left[0])
    arrived = [right_environment] + first + second
    near, far_mixed, low, high = middle_products(info, psi, lefts, arrived)
    low = lax.ppermute(low, "z", [(i, (i + 1) % Z) for i in range(Z)])
    high = lax.ppermute(high, "z", [(i, (i - 1) % Z) for i in range(Z)])
    far = far_products(info, far_mixed, third)
    far, near = tie((far, exchange(near)))
    sectors = [g[:, :, -1, 0].reshape(-1).astype(jnp.int32) for g in (low, high)]
    sectors = jnp.concatenate(sectors + [way[None].astype(jnp.int32)])
    guests = guest_products(sectors, low, high, third)
    guests, far = tie((guests, exchange(far)))
    guests = add_up(exchange(guests))
    flat = lambda part: part.reshape((-1,) + part.shape[2:])
    column, at = slot[0] // SLOTS, slot[0] % SLOTS
    first_far, first_end = 5 * CAP, 7 * CAP
    near, far = flat(add_up(near)), flat(add_up(far))
    place = jnp.where(
        at < first_far,
        column * first_far + at,
        near.shape[0] + column * (first_end - first_far) + at - first_far,
    )
    settled = settle(jnp.where(at < first_end, place, -1), (near, far))
    guests, settled = tie((guests, settled))
    home = [
        (i * Y + j, (i + (-1 if j < Y // 2 else 1)) % Z * Y + j) for i in range(Z) for j in range(Y)
    ]
    end = lax.ppermute(guests, ("z", "y"), home)

    hit = (at >= first_end) & (
        column * CAP + at - first_end == jnp.arange(Y * CAP, dtype=jnp.int32)[:, None]
    )
    target = jnp.max(jnp.where(hit, index, -1), axis=1)
    return finish(target, flat(end), settled)


def solution(mesh):
    fine = Mesh(mesh.devices.reshape(Z, Y, X, C), ("z", "y", "x", "c"))
    bond = ("z", "y")
    placed = (
        P(bond, None, None),
        P(("x", "c"), bond, None, None),
        P(("x", "c"), bond, None, None),
        P(bond),
    )
    return jax.shard_map(
        on_device, mesh=fine, in_specs=placed, out_specs=P(bond, ("x", "c"), None), check_vma=False
    )
```

```python
import functools

import jax
import jax.numpy as jnp
from jax import lax
from jax.experimental import pallas as pl
from jax.experimental.pallas import tpu as pltpu
from jax.sharding import Mesh, PartitionSpec as P

Z, Y, X, C = 8, 4, 4, 2
M = X * C
CAP = 3
SLOTS = Z * CAP
OFFSETS = (0, -1, 1, -2, 2, -3, 3, 4)
RANK = tuple(OFFSETS.index(((d + 3) % Z) - 3) for d in range(Z))
TILE = 16
MIRROR = tuple(OFFSETS.index(-d if -d in OFFSETS else d) for d in OFFSETS)
PSI_ORDER = (0, 1, 2, 7, 3, 4, 5, 6)


def ring(size, way):
    return [
        (i * C + c, (i + (way if c == 0 else -way)) % size * C + c)
        for i in range(size)
        for c in range(C)
    ]


def left_products(blocks, psi):
    terms, width = blocks.shape[0], blocks.shape[-1]
    mixed = jnp.dot(
        blocks.reshape(terms * width, width), psi, preferred_element_type=jnp.float32
    ).astype(jnp.bfloat16)
    return jnp.concatenate([mixed[w * width : (w + 1) * width] for w in range(terms)], axis=1)


def times_right(mixed, chosen):
    total = lax.dot_general(
        mixed,
        jnp.concatenate([chosen[w, 0] for w in range(chosen.shape[0])], axis=1),
        (((1,), (1,)), ((), ())),
        preferred_element_type=jnp.float32,
    )
    width = total.shape[0]
    return total.astype(jnp.bfloat16).reshape(M, width // M, width)


def left_products_turned(blocks, psi):
    terms, width = blocks.shape[0], blocks.shape[-1]
    mixed = jnp.dot(
        blocks.reshape(terms * width, width), psi, preferred_element_type=jnp.float32
    )
    turned = [mixed[w * width : (w + 1) * width].T for w in range(terms)]
    return jnp.concatenate(turned, axis=0).astype(jnp.bfloat16)


def right_times(chosen, turned):
    wide = jnp.concatenate([chosen[w, 0] for w in range(chosen.shape[0])], axis=1)
    total = jnp.dot(wide, turned, preferred_element_type=jnp.float32).astype(jnp.bfloat16).T
    width = total.shape[0]
    return total.reshape(M, width // M, width)


def middle_kernel(near, info_ref, *refs):
    psi, lefts, rights = refs[:C], refs[C : C + Y], refs[C + Y : C + Y + near]
    near_ref, far_ref, low_ref, high_ref, left, right, left_sems, right_sems = refs[C + Y + near :]
    home = pl.program_id(0)
    far = far_ref.shape[1] // CAP

    def left_copy(source, sector, i):
        return pltpu.make_async_copy(source.at[:, pl.ds(sector, 1)], left.at[i], left_sems.at[i])

    def right_copy(source, sector, i):
        return pltpu.make_async_copy(source.at[:, pl.ds(sector, 1)], right.at[i], right_sems.at[i])

    def start_home(h, carry):
        apart = (Y + info_ref[Y * SLOTS + 1] * (h - info_ref[Y * SLOTS])) % Y
        for n, source in enumerate(lefts):

            @pl.when(apart == n)
            def _(source=source):
                for q in range(SLOTS):
                    left_copy(source, info_ref[h * SLOTS + q] // 16, h * SLOTS + q).start()

        for q in range(near * CAP):
            sector = info_ref[h * SLOTS + q] % 16
            right_copy(rights[q // CAP], sector, h * near * CAP + q).start()
        return carry

    @pl.when(home == 0)
    def _():
        lax.fori_loop(0, Y, start_home, 0)

    for q in range(SLOTS):
        left_copy(lefts[0], 0, home * SLOTS + q).wait()
    for q in range(near * CAP):
        right_copy(rights[0], 0, home * near * CAP + q).wait()
    half = Z // C
    flipped = (1 - info_ref[Y * SLOTS + 1]) // 2
    for q in range(SLOTS):
        p, c = divmod(q, CAP)
        part, at = divmod(PSI_ORDER.index(p), half)
        shift = PSI_ORDER.index(MIRROR[p]) % half - at
        blocks = left[home * SLOTS + q, :, 0]
        mine = psi[part][0, at * CAP + c + flipped * (shift * CAP)]
        if q < near * CAP:
            chosen = right[home * near * CAP + q]
            to = q + flipped * ((MIRROR[p] - p) * CAP)
            near_ref[0, :, pl.ds(to, 1)] = times_right(left_products(blocks, mine), chosen)[:, None]
        elif q < (near + far) * CAP:
            far_ref[0, q - near * CAP] = left_products_turned(blocks, mine)
        else:
            turned = left_products_turned(blocks, mine)
            sector = info_ref[home * SLOTS + q] % 16
            tile = jnp.full((TILE, turned.shape[1]), sector, jnp.int32).astype(jnp.float32)
            turned = jnp.concatenate([turned, tile.astype(jnp.bfloat16)], axis=0)

            @pl.when(home < Y // 2)
            def _(turned=turned, i=q - (near + far) * CAP):
                low_ref[0, i] = turned

            @pl.when(home >= Y // 2)
            def _(turned=turned, i=q - (near + far) * CAP):
                high_ref[0, i] = turned


def far_kernel(count, info_ref, mixed_ref, *refs):
    rights, (out_ref, held, held_mixed, sems, mixed_sems) = refs[:count], refs[count:]
    flipped = (1 - info_ref[Y * SLOTS + 1]) // 2
    copies = []
    mixed_copies = [
        pltpu.make_async_copy(mixed_ref.at[h], held_mixed.at[h], mixed_sems.at[h])
        for h in range(Y)
    ]
    for h in range(Y):
        for s in range(count * CAP):
            place = s // CAP
            sector = info_ref[h * SLOTS + (Z - 1 - count) * CAP + s] % 16
            copies.append(
                pltpu.make_async_copy(
                    rights[place].at[:, pl.ds(sector, 1)],
                    held.at[h * count * CAP + s],
                    sems.at[h * count * CAP + s],
                )
            )
    for h in range(Y):
        mixed_copies[h].start()
        for copy in copies[h * count * CAP : (h + 1) * count * CAP]:
            copy.start()
    for h in range(Y):
        slots = range(h * count * CAP, (h + 1) * count * CAP)
        mixed_copies[h].wait()
        for i in slots:
            copies[i].wait()
        for s, i in enumerate(slots):
            to = s + flipped * (CAP if s < CAP else -CAP)
            out_ref[h, :, pl.ds(to, 1)] = right_times(held[i], held_mixed[h, s])[:, None]


def guest_kernel(index_ref, low_ref, high_ref, one_ref, other_ref, out_ref):
    rows = low_ref.shape[2] - TILE

    def products(low_source, high_source):
        for h in range(Y):
            guests, source = (low_ref, low_source) if h < Y // 2 else (high_ref, high_source)
            for s in range(CAP):
                chosen = source[:, pl.ds(index_ref[h * CAP + s], 1)]
                out_ref[h, :, s] = right_times(chosen, guests[h % (Y // 2), s, :rows])

    @pl.when(index_ref[Y * CAP] == 1)
    def _():
        products(other_ref, one_ref)

    @pl.when(index_ref[Y * CAP] != 1)
    def _():
        products(one_ref, other_ref)


MIDDLE = pltpu.CompilerParams(vmem_limit_bytes=56 * 1024 * 1024)
LARGE = pltpu.CompilerParams(vmem_limit_bytes=60 * 1024 * 1024)


def cost(slots, matmuls, terms, width):
    return pl.CostEstimate(
        flops=2 * slots * matmuls * terms * width**3,
        bytes_accessed=slots * (matmuls * terms + 2) * width * width * 2,
        transcendentals=0,
    )


def middle_products(info, psi, lefts, rights):
    terms, _, width, _ = lefts[0].shape
    near, far = len(rights), Z - 1 - len(rights)
    one = (terms, 1, width, width)
    turned = jax.ShapeDtypeStruct((Y, far * CAP, terms * width, width), jnp.bfloat16)
    guest = jax.ShapeDtypeStruct((Y // 2, CAP, terms * width + TILE, width), jnp.bfloat16)
    out = jax.ShapeDtypeStruct((Y, M, near * CAP, width // M, width), jnp.bfloat16)
    per_home = lambda shape: pl.BlockSpec(
        (1,) + shape[1:], lambda h, info: (h,) + (0,) * (len(shape) - 1)
    )
    return pl.pallas_call(
        functools.partial(middle_kernel, near),
        out_shape=[out, turned, guest, guest],
        grid_spec=pltpu.PrefetchScalarGridSpec(
            num_scalar_prefetch=1,
            grid=(Y,),
            in_specs=[per_home(p.shape) for p in psi]
            + [pl.BlockSpec(memory_space=pl.ANY)] * (len(lefts) + near),
            out_specs=[
                per_home(out.shape),
                per_home(turned.shape),
                pl.BlockSpec(
                    (1,) + guest.shape[1:],
                    lambda h, info: (jnp.minimum(h, Y // 2 - 1), 0, 0, 0),
                ),
                pl.BlockSpec(
                    (1,) + guest.shape[1:],
                    lambda h, info: (jnp.maximum(h - Y // 2, 0), 0, 0, 0),
                ),
            ],
            scratch_shapes=[
                pltpu.VMEM((Y * SLOTS,) + one, jnp.bfloat16),
                pltpu.VMEM((Y * near * CAP,) + one, jnp.bfloat16),
                pltpu.SemaphoreType.DMA((Y * SLOTS,)),
                pltpu.SemaphoreType.DMA((Y * near * CAP,)),
            ],
        ),
        compiler_params=LARGE,
        cost_estimate=cost(Y * SLOTS, 2, terms, width),
    )(info, *psi, *lefts, *rights)


SMALL = pltpu.CompilerParams(vmem_limit_bytes=24 * 1024 * 1024)
IN_VMEM = pl.BlockSpec(memory_space=pltpu.VMEM)
IN_HBM = pl.BlockSpec(memory_space=pltpu.HBM)


def far_products(info, mixed, arrived):
    slots, width = mixed.shape[1], mixed.shape[3]
    terms = mixed.shape[2] // width
    return pl.pallas_call(
        functools.partial(far_kernel, len(arrived)),
        out_shape=jax.ShapeDtypeStruct((Y, M, slots, width // M, width), jnp.bfloat16),
        in_specs=[pl.BlockSpec(memory_space=pltpu.SMEM)] + [IN_HBM] * (1 + len(arrived)),
        out_specs=IN_VMEM,
        scratch_shapes=[
            pltpu.VMEM((Y * slots, terms, 1, width, width), jnp.bfloat16),
            pltpu.VMEM(mixed.shape, jnp.bfloat16),
            pltpu.SemaphoreType.DMA((Y * slots,)),
            pltpu.SemaphoreType.DMA((Y,)),
        ],
        compiler_params=MIDDLE,
        cost_estimate=cost(Y * slots, 2, terms, width),
    )(info, mixed, *arrived)


def guest_products(index, low, high, arrived):
    terms, _, width, _ = arrived[0].shape
    return pl.pallas_call(
        guest_kernel,
        out_shape=jax.ShapeDtypeStruct((Y, M, CAP, width // M, width), jnp.bfloat16),
        in_specs=[pl.BlockSpec(memory_space=pltpu.SMEM)] + [IN_VMEM] * 4,
        out_specs=IN_VMEM,
        compiler_params=SMALL,
        cost_estimate=cost(Y * CAP, 2, terms, width),
    )(index, low, high, *arrived)


def settle_kernel(place_ref, *refs):
    parts, out_ref = refs[:-1], refs[-1]
    starts = [0]
    for part in parts:
        starts.append(starts[-1] + part.shape[0])
    for k in range(out_ref.shape[0]):
        place = place_ref[k]
        for n, part in enumerate(parts):

            @pl.when((place >= starts[n]) & (place < starts[n + 1]))
            def _(k=k, part=part, start=starts[n], place=place):
                out_ref[k] = part[place - start]


def settle(place, parts):
    return pl.pallas_call(
        settle_kernel,
        out_shape=jax.ShapeDtypeStruct(place.shape + parts[0].shape[1:], parts[0].dtype),
        in_specs=[pl.BlockSpec(memory_space=pltpu.SMEM)] + [IN_VMEM] * len(parts),
        out_specs=IN_VMEM,
        compiler_params=SMALL,
    )(place, *parts)


def finish_kernel(target_ref, end_ref, settled_ref, out_ref, sems):
    del settled_ref
    copies = [
        pltpu.make_async_copy(
            end_ref.at[i], out_ref.at[jnp.maximum(target_ref[i], 0)], sems.at[i]
        )
        for i in range(end_ref.shape[0])
    ]
    for i, copy in enumerate(copies):
        pl.when(target_ref[i] >= 0)(copy.start)
    for i, copy in enumerate(copies):
        pl.when(target_ref[i] >= 0)(copy.wait)


def finish(target, end, settled):
    return pl.pallas_call(
        finish_kernel,
        out_shape=jax.ShapeDtypeStruct(settled.shape, settled.dtype),
        in_specs=[pl.BlockSpec(memory_space=pltpu.SMEM), IN_VMEM, IN_HBM],
        out_specs=IN_HBM,
        scratch_shapes=[pltpu.SemaphoreType.DMA(target.shape)],
        input_output_aliases={2: 0},
        compiler_params=SMALL,
    )(target, end, settled)


def exchange(part):
    part = part.reshape((Y * M,) + part.shape[2:])
    part = lax.all_to_all(part, ("y", "x", "c"), split_axis=0, concat_axis=0, tiled=True)
    return part.reshape((Y, M) + part.shape[1:])


def add_up(part):
    return part.astype(jnp.float32).sum(axis=1).astype(jnp.bfloat16)


def on_device(wavefunction, left_environment, right_environment, right_sector):
    z, y, core = (lax.axis_index(name) for name in ("z", "y", "c"))
    blocks, width = wavefunction.shape[:2]
    owned = left_environment.shape[1]
    members = blocks // owned
    tie = lax.optimization_barrier

    way = 1 - 2 * core

    def hop(moved, axis, direction):
        size = Z if axis == "z" else Y
        return lax.ppermute(moved, (axis, "c"), ring(size, direction))

    def step(moving, axis="z"):
        return [hop(moving[0], axis, 1), hop(moving[1], axis, -1)]

    first = step([right_environment] * 2)

    index = jnp.arange(blocks, dtype=jnp.int32)
    earlier = index[None, :] < index[:, None]

    def slots_of(sectors, direction):
        owner = sectors // owned
        same = owner[:, :, None] == owner[:, None, :]
        place = jnp.sum((same & earlier).astype(jnp.int32), axis=2)
        offset = (direction * (owner // Y - z)) % Z
        rank = sum(jnp.where(offset == d, RANK[d], 0) for d in range(Z))
        return owner % Y, rank * CAP + place

    def into(slots, values, count):
        hit = slots[:, None, :] == jnp.arange(count, dtype=jnp.int32)[None, :, None]
        return jnp.sum(jnp.where(hit, values[:, None, :], 0), axis=2)

    column, slot = slots_of(right_sector[None], 1)
    slot = column * SLOTS + slot
    split = SLOTS // C
    rank = (slot % SLOTS) // CAP
    position = sum(jnp.where(rank == p, n, 0) for n, p in enumerate(PSI_ORDER)) * CAP + slot % CAP
    mine = column * split + jnp.where(position // split == core, position % split, -Y * SLOTS)
    source = into(mine, index[None], Y * split)[0]
    outgoing = wavefunction.at[source].get(mode="promise_in_bounds")
    outgoing = outgoing.reshape((Y, split) + wavefunction.shape[1:])

    sectors = jnp.broadcast_to(right_sector, (Y, blocks))
    sectors = lax.all_to_all(sectors, "y", split_axis=0, concat_axis=0, tiled=True)
    left_environment, sectors = tie((left_environment, sectors))
    near_left = step([left_environment] * 2, "y")
    column, here = slots_of(sectors, way)
    here = jnp.where(column == y, here, -1)
    info = into(here, (index // members) * 16 + sectors % owned, SLOTS)
    info = jnp.concatenate([info.reshape(-1), jnp.stack([y, way]).astype(jnp.int32)])

    second = step(first)
    psi = lax.all_to_all(outgoing, "y", split_axis=0, concat_axis=0, tiled=True)
    far_left = hop(near_left[0], "y", 1)
    other = lax.ppermute(psi, "c", [(0, 1), (1, 0)])
    psi = (jnp.where(core == 0, psi, other), jnp.where(core == 0, other, psi))
    second, psi = tie((second, psi))
    third = step(second)
    lefts = (left_environment, near_left[1], far_left, near_left[0])
    arrived = [right_environment] + first + second
    near, far_mixed, low, high = middle_products(info, psi, lefts, arrived)
    low = lax.ppermute(low, "z", [(i, (i + 1) % Z) for i in range(Z)])
    high = lax.ppermute(high, "z", [(i, (i - 1) % Z) for i in range(Z)])
    far = far_products(info, far_mixed, third)
    far, near = tie((far, exchange(near)))
    sectors = [g[:, :, -1, 0].reshape(-1).astype(jnp.int32) for g in (low, high)]
    sectors = jnp.concatenate(sectors + [way[None].astype(jnp.int32)])
    guests = guest_products(sectors, low, high, third)
    guests, far = tie((guests, exchange(far)))
    guests = add_up(exchange(guests))
    flat = lambda part: part.reshape((-1,) + part.shape[2:])
    column, at = slot[0] // SLOTS, slot[0] % SLOTS
    first_far, first_end = 5 * CAP, 7 * CAP
    near, far = flat(add_up(near)), flat(add_up(far))
    place = jnp.where(
        at < first_far,
        column * first_far + at,
        near.shape[0] + column * (first_end - first_far) + at - first_far,
    )
    settled = settle(jnp.where(at < first_end, place, -1), (near, far))
    guests, settled = tie((guests, settled))
    home = [
        (i * Y + j, (i + (-1 if j < Y // 2 else 1)) % Z * Y + j) for i in range(Z) for j in range(Y)
    ]
    end = lax.ppermute(guests, ("z", "y"), home)

    hit = (at >= first_end) & (
        column * CAP + at - first_end == jnp.arange(Y * CAP, dtype=jnp.int32)[:, None]
    )
    target = jnp.max(jnp.where(hit, index, -1), axis=1)
    return finish(target, flat(end), settled)


def solution(mesh):
    fine = Mesh(mesh.devices.reshape(Z, Y, X, C), ("z", "y", "x", "c"))
    bond = ("z", "y")
    placed = (
        P(bond, None, None),
        P(("x", "c"), bond, None, None),
        P(("x", "c"), bond, None, None),
        P(bond),
    )
    return jax.shard_map(
        on_device, mesh=fine, in_specs=placed, out_specs=P(bond, ("x", "c"), None), check_vma=False
    )
```

```python
import functools

import jax
import jax.numpy as jnp
from jax import lax
from jax.experimental import pallas as pl
from jax.experimental.pallas import tpu as pltpu
from jax.sharding import Mesh, PartitionSpec as P

Z, Y, X, C = 8, 4, 4, 2
M = X * C
CAP = 3
SLOTS = Z * CAP
OFFSETS = (0, -1, 1, -2, 2, -3, 3, 4)
RANK = tuple(OFFSETS.index(((d + 3) % Z) - 3) for d in range(Z))
TILE = 16
MIRROR = tuple(OFFSETS.index(-d if -d in OFFSETS else d) for d in OFFSETS)
PSI_ORDER = (0, 1, 2, 7, 3, 4, 5, 6)


def ring(size, way):
    return [
        (i * C + c, (i + (way if c == 0 else -way)) % size * C + c)
        for i in range(size)
        for c in range(C)
    ]


def left_products(blocks, psi):
    terms, width = blocks.shape[0], blocks.shape[-1]
    mixed = jnp.dot(
        blocks.reshape(terms * width, width), psi, preferred_element_type=jnp.float32
    ).astype(jnp.bfloat16)
    return jnp.concatenate([mixed[w * width : (w + 1) * width] for w in range(terms)], axis=1)


def times_right(mixed, chosen):
    total = lax.dot_general(
        mixed,
        jnp.concatenate([chosen[w, 0] for w in range(chosen.shape[0])], axis=1),
        (((1,), (1,)), ((), ())),
        preferred_element_type=jnp.float32,
    )
    width = total.shape[0]
    return total.astype(jnp.bfloat16).reshape(M, width // M, width)


def left_products_turned(blocks, psi):
    terms, width = blocks.shape[0], blocks.shape[-1]
    mixed = jnp.dot(
        blocks.reshape(terms * width, width), psi, preferred_element_type=jnp.float32
    )
    turned = [mixed[w * width : (w + 1) * width].T for w in range(terms)]
    return jnp.concatenate(turned, axis=0).astype(jnp.bfloat16)


def right_times(chosen, turned):
    wide = jnp.concatenate([chosen[w, 0] for w in range(chosen.shape[0])], axis=1)
    total = jnp.dot(wide, turned, preferred_element_type=jnp.float32).astype(jnp.bfloat16).T
    width = total.shape[0]
    return total.reshape(M, width // M, width)


def middle_kernel(near, info_ref, *refs):
    psi, lefts, rights = refs[:C], refs[C : C + Y], refs[C + Y : C + Y + near]
    near_ref, far_ref, low_ref, high_ref, left, right, left_sems, right_sems = refs[C + Y + near :]
    home = pl.program_id(0)
    far = far_ref.shape[1] // CAP

    def left_copy(source, sector, i):
        return pltpu.make_async_copy(source.at[:, pl.ds(sector, 1)], left.at[i], left_sems.at[i])

    def right_copy(source, sector, i):
        return pltpu.make_async_copy(source.at[:, pl.ds(sector, 1)], right.at[i], right_sems.at[i])

    def start_home(h, carry):
        apart = (Y + info_ref[Y * SLOTS + 1] * (h - info_ref[Y * SLOTS])) % Y
        for n, source in enumerate(lefts):

            @pl.when(apart == n)
            def _(source=source):
                for q in range(SLOTS):
                    left_copy(source, info_ref[h * SLOTS + q] // 16, h * SLOTS + q).start()

        for q in range(near * CAP):
            sector = info_ref[h * SLOTS + q] % 16
            right_copy(rights[q // CAP], sector, h * near * CAP + q).start()
        return carry

    @pl.when(home == 0)
    def _():
        lax.fori_loop(0, Y, start_home, 0)

    for q in range(SLOTS):
        left_copy(lefts[0], 0, home * SLOTS + q).wait()
    for q in range(near * CAP):
        right_copy(rights[0], 0, home * near * CAP + q).wait()
    half = Z // C
    flipped = (1 - info_ref[Y * SLOTS + 1]) // 2
    for q in range(SLOTS):
        p, c = divmod(q, CAP)
        part, at = divmod(PSI_ORDER.index(p), half)
        shift = PSI_ORDER.index(MIRROR[p]) % half - at
        blocks = left[home * SLOTS + q, :, 0]
        mine = psi[part][0, at * CAP + c + flipped * (shift * CAP)]
        if q < near * CAP:
            chosen = right[home * near * CAP + q]
            to = q + flipped * ((MIRROR[p] - p) * CAP)
            near_ref[0, :, pl.ds(to, 1)] = times_right(left_products(blocks, mine), chosen)[:, None]
        elif q < (near + far) * CAP:
            far_ref[0, q - near * CAP] = left_products_turned(blocks, mine)
        else:
            turned = left_products_turned(blocks, mine)
            sector = info_ref[home * SLOTS + q] % 16
            tile = jnp.full((TILE, turned.shape[1]), sector, jnp.int32).astype(jnp.float32)
            turned = jnp.concatenate([turned, tile.astype(jnp.bfloat16)], axis=0)

            @pl.when(home < Y // 2)
            def _(turned=turned, i=q - (near + far) * CAP):
                low_ref[0, i] = turned

            @pl.when(home >= Y // 2)
            def _(turned=turned, i=q - (near + far) * CAP):
                high_ref[0, i] = turned


def far_kernel(count, info_ref, mixed_ref, *refs):
    rights, (keep_ref, give_ref, held, held_mixed, sems, mixed_sems) = refs[:count], refs[count:]
    flipped = (1 - info_ref[Y * SLOTS + 1]) // 2
    copies = []
    mixed_copies = [
        pltpu.make_async_copy(mixed_ref.at[h], held_mixed.at[h], mixed_sems.at[h])
        for h in range(Y)
    ]
    for h in range(Y):
        for s in range(count * CAP):
            place = s // CAP
            sector = info_ref[h * SLOTS + (Z - 1 - count) * CAP + s] % 16
            copies.append(
                pltpu.make_async_copy(
                    rights[place].at[:, pl.ds(sector, 1)],
                    held.at[h * count * CAP + s],
                    sems.at[h * count * CAP + s],
                )
            )
    for h in range(Y):
        mixed_copies[h].start()
        for copy in copies[h * count * CAP : (h + 1) * count * CAP]:
            copy.start()
    for h in range(Y):
        slots = range(h * count * CAP, (h + 1) * count * CAP)
        mixed_copies[h].wait()
        for i in slots:
            copies[i].wait()
        for s, i in enumerate(slots):
            to = s + flipped * (CAP if s < CAP else -CAP)
            total = right_times(held[i], held_mixed[h, s])
            total = total.reshape((X, C) + total.shape[1:])
            keep_ref[h, :, pl.ds(to, 1)] = jnp.where(flipped == 0, total[:, 0], total[:, 1])[:, None]
            give_ref[h, :, pl.ds(to, 1)] = jnp.where(flipped == 0, total[:, 1], total[:, 0])[:, None]


def guest_kernel(index_ref, low_ref, high_ref, one_ref, other_ref, out_ref):
    rows = low_ref.shape[2] - TILE

    def products(low_source, high_source):
        for h in range(Y):
            guests, source = (low_ref, low_source) if h < Y // 2 else (high_ref, high_source)
            for s in range(CAP):
                chosen = source[:, pl.ds(index_ref[h * CAP + s], 1)]
                out_ref[h, :, s] = right_times(chosen, guests[h % (Y // 2), s, :rows])

    @pl.when(index_ref[Y * CAP] == 1)
    def _():
        products(other_ref, one_ref)

    @pl.when(index_ref[Y * CAP] != 1)
    def _():
        products(one_ref, other_ref)


MIDDLE = pltpu.CompilerParams(vmem_limit_bytes=56 * 1024 * 1024)
LARGE = pltpu.CompilerParams(vmem_limit_bytes=60 * 1024 * 1024)


def cost(slots, matmuls, terms, width):
    return pl.CostEstimate(
        flops=2 * slots * matmuls * terms * width**3,
        bytes_accessed=slots * (matmuls * terms + 2) * width * width * 2,
        transcendentals=0,
    )


def middle_products(info, psi, lefts, rights):
    terms, _, width, _ = lefts[0].shape
    near, far = len(rights), Z - 1 - len(rights)
    one = (terms, 1, width, width)
    turned = jax.ShapeDtypeStruct((Y, far * CAP, terms * width, width), jnp.bfloat16)
    guest = jax.ShapeDtypeStruct((Y // 2, CAP, terms * width + TILE, width), jnp.bfloat16)
    out = jax.ShapeDtypeStruct((Y, M, near * CAP, width // M, width), jnp.bfloat16)
    per_home = lambda shape: pl.BlockSpec(
        (1,) + shape[1:], lambda h, info: (h,) + (0,) * (len(shape) - 1)
    )
    return pl.pallas_call(
        functools.partial(middle_kernel, near),
        out_shape=[out, turned, guest, guest],
        grid_spec=pltpu.PrefetchScalarGridSpec(
            num_scalar_prefetch=1,
            grid=(Y,),
            in_specs=[per_home(p.shape) for p in psi]
            + [pl.BlockSpec(memory_space=pl.ANY)] * (len(lefts) + near),
            out_specs=[
                per_home(out.shape),
                per_home(turned.shape),
                pl.BlockSpec(
                    (1,) + guest.shape[1:],
                    lambda h, info: (jnp.minimum(h, Y // 2 - 1), 0, 0, 0),
                ),
                pl.BlockSpec(
                    (1,) + guest.shape[1:],
                    lambda h, info: (jnp.maximum(h - Y // 2, 0), 0, 0, 0),
                ),
            ],
            scratch_shapes=[
                pltpu.VMEM((Y * SLOTS,) + one, jnp.bfloat16),
                pltpu.VMEM((Y * near * CAP,) + one, jnp.bfloat16),
                pltpu.SemaphoreType.DMA((Y * SLOTS,)),
                pltpu.SemaphoreType.DMA((Y * near * CAP,)),
            ],
        ),
        compiler_params=LARGE,
        cost_estimate=cost(Y * SLOTS, 2, terms, width),
    )(info, *psi, *lefts, *rights)


SMALL = pltpu.CompilerParams(vmem_limit_bytes=24 * 1024 * 1024)
IN_VMEM = pl.BlockSpec(memory_space=pltpu.VMEM)
IN_HBM = pl.BlockSpec(memory_space=pltpu.HBM)


def far_products(info, mixed, arrived):
    slots, width = mixed.shape[1], mixed.shape[3]
    terms = mixed.shape[2] // width
    out = jax.ShapeDtypeStruct((Y, X, slots, width // M, width), jnp.bfloat16)
    return pl.pallas_call(
        functools.partial(far_kernel, len(arrived)),
        out_shape=[out, out],
        in_specs=[pl.BlockSpec(memory_space=pltpu.SMEM)] + [IN_HBM] * (1 + len(arrived)),
        out_specs=[IN_VMEM, IN_VMEM],
        scratch_shapes=[
            pltpu.VMEM((Y * slots, terms, 1, width, width), jnp.bfloat16),
            pltpu.VMEM(mixed.shape, jnp.bfloat16),
            pltpu.SemaphoreType.DMA((Y * slots,)),
            pltpu.SemaphoreType.DMA((Y,)),
        ],
        compiler_params=MIDDLE,
        cost_estimate=cost(Y * slots, 2, terms, width),
    )(info, mixed, *arrived)


def guest_products(index, low, high, arrived):
    terms, _, width, _ = arrived[0].shape
    return pl.pallas_call(
        guest_kernel,
        out_shape=jax.ShapeDtypeStruct((Y, M, CAP, width // M, width), jnp.bfloat16),
        in_specs=[pl.BlockSpec(memory_space=pltpu.SMEM)] + [IN_VMEM] * 4,
        out_specs=IN_VMEM,
        compiler_params=SMALL,
        cost_estimate=cost(Y * CAP, 2, terms, width),
    )(index, low, high, *arrived)


def settle_kernel(place_ref, *refs):
    parts, out_ref = refs[:-1], refs[-1]
    starts = [0]
    for part in parts:
        starts.append(starts[-1] + part.shape[0])
    for k in range(out_ref.shape[0]):
        place = place_ref[k]
        for n, part in enumerate(parts):

            @pl.when((place >= starts[n]) & (place < starts[n + 1]))
            def _(k=k, part=part, start=starts[n], place=place):
                out_ref[k] = part[place - start]


def settle(place, parts):
    return pl.pallas_call(
        settle_kernel,
        out_shape=jax.ShapeDtypeStruct(place.shape + parts[0].shape[1:], parts[0].dtype),
        in_specs=[pl.BlockSpec(memory_space=pltpu.SMEM)] + [IN_VMEM] * len(parts),
        out_specs=IN_VMEM,
        compiler_params=SMALL,
    )(place, *parts)


def finish_kernel(target_ref, end_ref, settled_ref, out_ref, sems):
    del settled_ref
    copies = [
        pltpu.make_async_copy(
            end_ref.at[i], out_ref.at[jnp.maximum(target_ref[i], 0)], sems.at[i]
        )
        for i in range(end_ref.shape[0])
    ]
    for i, copy in enumerate(copies):
        pl.when(target_ref[i] >= 0)(copy.start)
    for i, copy in enumerate(copies):
        pl.when(target_ref[i] >= 0)(copy.wait)


def finish(target, end, settled):
    return pl.pallas_call(
        finish_kernel,
        out_shape=jax.ShapeDtypeStruct(settled.shape, settled.dtype),
        in_specs=[pl.BlockSpec(memory_space=pltpu.SMEM), IN_VMEM, IN_HBM],
        out_specs=IN_HBM,
        scratch_shapes=[pltpu.SemaphoreType.DMA(target.shape)],
        input_output_aliases={2: 0},
        compiler_params=SMALL,
    )(target, end, settled)


def exchange(part, axes=("y", "x", "c")):
    shape = part.shape
    part = part.reshape((-1,) + shape[2:])
    part = lax.all_to_all(part, axes, split_axis=0, concat_axis=0, tiled=True)
    return part.reshape(shape)


def add_up(part):
    return part.astype(jnp.float32).sum(axis=1).astype(jnp.bfloat16)


def on_device(wavefunction, left_environment, right_environment, right_sector):
    z, y, core = (lax.axis_index(name) for name in ("z", "y", "c"))
    blocks, width = wavefunction.shape[:2]
    owned = left_environment.shape[1]
    members = blocks // owned
    tie = lax.optimization_barrier

    way = 1 - 2 * core

    def hop(moved, axis, direction):
        size = Z if axis == "z" else Y
        return lax.ppermute(moved, (axis, "c"), ring(size, direction))

    def step(moving, axis="z"):
        return [hop(moving[0], axis, 1), hop(moving[1], axis, -1)]

    first = step([right_environment] * 2)

    index = jnp.arange(blocks, dtype=jnp.int32)
    earlier = index[None, :] < index[:, None]

    def slots_of(sectors, direction):
        owner = sectors // owned
        same = owner[:, :, None] == owner[:, None, :]
        place = jnp.sum((same & earlier).astype(jnp.int32), axis=2)
        offset = (direction * (owner // Y - z)) % Z
        rank = sum(jnp.where(offset == d, RANK[d], 0) for d in range(Z))
        return owner % Y, rank * CAP + place

    def into(slots, values, count):
        hit = slots[:, None, :] == jnp.arange(count, dtype=jnp.int32)[None, :, None]
        return jnp.sum(jnp.where(hit, values[:, None, :], 0), axis=2)

    column, slot = slots_of(right_sector[None], 1)
    slot = column * SLOTS + slot
    split = SLOTS // C
    rank = (slot % SLOTS) // CAP
    position = sum(jnp.where(rank == p, n, 0) for n, p in enumerate(PSI_ORDER)) * CAP + slot % CAP
    mine = column * split + jnp.where(position // split == core, position % split, -Y * SLOTS)
    source = into(mine, index[None], Y * split)[0]
    outgoing = wavefunction.at[source].get(mode="promise_in_bounds")
    outgoing = outgoing.reshape((Y, split) + wavefunction.shape[1:])

    sectors = jnp.broadcast_to(right_sector, (Y, blocks))
    sectors = lax.all_to_all(sectors, "y", split_axis=0, concat_axis=0, tiled=True)
    left_environment, sectors = tie((left_environment, sectors))
    near_left = step([left_environment] * 2, "y")
    column, here = slots_of(sectors, way)
    here = jnp.where(column == y, here, -1)
    info = into(here, (index // members) * 16 + sectors % owned, SLOTS)
    info = jnp.concatenate([info.reshape(-1), jnp.stack([y, way]).astype(jnp.int32)])

    second = step(first)
    psi = lax.all_to_all(outgoing, "y", split_axis=0, concat_axis=0, tiled=True)
    far_left = hop(near_left[0], "y", 1)
    other = lax.ppermute(psi, "c", [(0, 1), (1, 0)])
    psi = (jnp.where(core == 0, psi, other), jnp.where(core == 0, other, psi))
    second[1], psi = tie((second[1], psi))
    third = step(second)
    lefts = (left_environment, near_left[1], far_left, near_left[0])
    arrived = [right_environment] + first + second
    near, far_mixed, low, high = middle_products(info, psi, lefts, arrived)
    low = lax.ppermute(low, "z", [(i, (i + 1) % Z) for i in range(Z)])
    high = lax.ppermute(high, "z", [(i, (i - 1) % Z) for i in range(Z)])
    keep, give = far_products(info, far_mixed, third)
    given = lax.ppermute(give, "c", [(0, 1), (1, 0)])
    far = (keep.astype(jnp.float32) + given.astype(jnp.float32)).astype(jnp.bfloat16)
    far, near = tie((far, exchange(near)))
    sectors = [g[:, :, -1, 0].reshape(-1).astype(jnp.int32) for g in (low, high)]
    sectors = jnp.concatenate(sectors + [way[None].astype(jnp.int32)])
    guests = guest_products(sectors, low, high, third)
    guests, far = tie((guests, exchange(far, ("y", "x"))))
    guests = add_up(exchange(guests))
    flat = lambda part: part.reshape((-1,) + part.shape[2:])
    column, at = slot[0] // SLOTS, slot[0] % SLOTS
    first_far, first_end = 5 * CAP, 7 * CAP
    near, far = flat(add_up(near)), flat(add_up(far))
    place = jnp.where(
        at < first_far,
        column * first_far + at,
        near.shape[0] + column * (first_end - first_far) + at - first_far,
    )
    settled = settle(jnp.where(at < first_end, place, -1), (near, far))
    guests, settled = tie((guests, settled))
    home = [
        (i * Y + j, (i + (-1 if j < Y // 2 else 1)) % Z * Y + j) for i in range(Z) for j in range(Y)
    ]
    end = lax.ppermute(guests, ("z", "y"), home)

    hit = (at >= first_end) & (
        column * CAP + at - first_end == jnp.arange(Y * CAP, dtype=jnp.int32)[:, None]
    )
    target = jnp.max(jnp.where(hit, index, -1), axis=1)
    return finish(target, flat(end), settled)


def solution(mesh):
    fine = Mesh(mesh.devices.reshape(Z, Y, X, C), ("z", "y", "x", "c"))
    bond = ("z", "y")
    placed = (
        P(bond, None, None),
        P(("x", "c"), bond, None, None),
        P(("x", "c"), bond, None, None),
        P(bond),
    )
    return jax.shard_map(
        on_device, mesh=fine, in_specs=placed, out_specs=P(bond, ("x", "c"), None), check_vma=False
    )
```
